256 devices in a mesh: rows: 64 (over y, z_hi, x, core), heads: 4 (over z_lo).
Axes of the slice: x: 4, y: 4, z: 8 (z_hi: 2, z_lo: 4; z = z_hi * 4 + z_lo), core: 2. Of those that a mesh axis runs over, the one named last changes fastest.
Arguments:
- slab: bfloat16 [256, 1024, 128], P('rows'), may hold values from -6 to 6
- pair: bfloat16 [1024, 1024, 128], P('rows'), may hold values from -6 to 6
- pair_mask: int32 [256, 1024], P('rows'), may hold values from 0 to 1, as said below
- w_qkvg: bfloat16 [128, 4, 128], P(None, None, 'heads')
- w_out: bfloat16 [128, 128], P('heads'), may hold values from -0.5 to 0.5
- w_bias: bfloat16 [128, 4], replicated
- d_out: bfloat16 [256, 1024, 128], P('rows'), may hold values from -16 to 16
Outputs:
- d_slab: bfloat16 [256, 1024, 128], P('rows')
- d_pair: bfloat16 [1024, 1024, 128], P('rows', None, 'heads')
- d_wqkvg: float32 [128, 4, 128], P(None, None, 'heads')
- d_wout: float32 [128, 128], P('heads')
- d_wbias: float32 [128, 4], P(None, 'heads')
The draws below stay inside these ranges and needn't reach their ends.
Inputs may be any that keep to these rules, and one draw needn't show every extreme that they name: pair_mask[i, k] is the product of two residue flags, of residue i and residue k; the 1024 residues form 4 chains of 256, each ending in a run of padded residues of length 0 to half the chain (128); the first residue of every chain is real.
All inputs are finite; a program needn't handle non-finite values.
Results may differ from the reference program's by a relative error of at most 0.017.
The reference program's roundings to bfloat16 on the way count: a program that leaves them out, or rounds other values in their place, can miss the bound.
Values may be sent and summed in bfloat16 or wider, within the bound.
A program may use at most 128 MiB of HBM per device.

```python
import jax
import jax.numpy as jnp
from jax import lax

C = 128
DH = 32
H = 4
HD = 128
N = 1024
SLAB = 256


def draw_slab(key, part):
    key = jax.random.fold_in(key, 5)
    base = jax.random.normal(key, (SLAB, N, C), jnp.float32)
    return jnp.clip(base, -6.0, 6.0).astype(jnp.bfloat16)


def draw_w_qkvg(key, part):
    key = jax.random.fold_in(key, 9)
    base = jnp.clip(jax.random.normal(key, (C, 4, HD), jnp.float32), -6.0, 6.0)
    return (base / C ** 0.5).astype(jnp.bfloat16)


def draw_pair_mask(key, part):
    key = jax.random.fold_in(key, 7)
    length = N // 4
    padding = jax.random.randint(key, (4,), 0, length // 2 + 1)
    place = jnp.arange(N)
    chain = place // length
    within = place % length
    real = (within < length - padding[chain]).astype(jnp.int32)
    return real[:SLAB, None] * real[None, :]


def draw_w_bias(key, part):
    key = jax.random.fold_in(key, 11)
    base = jax.random.normal(key, (C, H), jnp.float32)
    return (base * 1.5 / C ** 0.5).astype(jnp.bfloat16)


def strengthened(entries, stream_key, source, target, parts, factor):
    owner, partner = [(jnp.arange(entries.shape[position]) // (entries.shape[position] // parts)).reshape([-1 if axis == position else 1 for axis in range(entries.ndim)]) for position in (source, target)]
    chosen = jax.random.permutation(stream_key, parts)[partner]
    strong = (owner == chosen) | (owner == (partner + parts // 2) % parts)
    return jnp.where(strong, factor * entries, entries)


def steps_of(own_key, extent, split, low, high):
    level, own = 1.0, jax.random.fold_in(own_key, 6)
    for position, parts in split:
        steps = jnp.exp(jax.random.uniform(jax.random.fold_in(own, position), (parts,), jnp.float32, low / len(split), high / len(split)))
        level = level * jnp.repeat(steps, extent[position] // parts).reshape([-1 if axis == position else 1 for axis in range(len(extent))])
    return level


def scatter_about(stream_key, shape, spread, bound, pieces=(), kind=jnp.bfloat16):
    factor_of = steps_of(stream_key, shape, pieces, -0.22, 0.18) if pieces else 1.0
    entries = jax.random.normal(stream_key, shape, jnp.float32) * spread * factor_of
    return jnp.minimum(jnp.maximum(entries, -bound), bound).astype(kind)


def bell_draw_with(stream_key, extent, spread, most, cuts, heavy, held_as=jnp.bfloat16):
    array = spread * jax.random.normal(stream_key, extent, jnp.float32)
    if cuts:
        array = array * steps_of(stream_key, extent, cuts, -0.22, 0.18)
    return jnp.clip(strengthened(array, jax.random.fold_in(stream_key, 3), *heavy), -most, most).astype(held_as)


def setup_inputs(seed: int = 0) -> dict:
    key_of = jax.random.split(jax.random.key(seed), 8)
    slab = draw_slab(jax.random.fold_in(key_of[7], 71), 0)
    pair = scatter_about(key_of[1], (N, N, C), 1.0, 6.0, ((0, 64),))
    pair_mask = draw_pair_mask(jax.random.fold_in(key_of[7], 71), 0)
    w_qkvg = draw_w_qkvg(jax.random.fold_in(key_of[7], 71), 0)
    w_out = scatter_about(key_of[4], (HD, C), HD ** -0.5, 0.5, ((0, 4),))
    w_bias = draw_w_bias(jax.random.fold_in(key_of[7], 71), 0)
    d_out = bell_draw_with(key_of[6], (SLAB, N, C), 1.0, 16.0, ((0, 64),), (0, 1, 64, 4.0))
    return {"slab": slab, "pair": pair, "pair_mask": pair_mask, "w_qkvg": w_qkvg, "w_out": w_out, "w_bias": w_bias, "d_out": d_out}


def norm_stats(tensor):
    full = tensor.astype(jnp.float32)
    center = full - lax.optimization_barrier(jnp.mean(full, axis=-1, keepdims=True))
    recip = lax.rsqrt(lax.optimization_barrier(jnp.mean(center * center, axis=-1, keepdims=True)) + 1e-05)
    return (center * recip, recip)

def norm_back(normed, recip, grad):
    first = lax.optimization_barrier(jnp.mean(grad, axis=-1, keepdims=True))
    second = lax.optimization_barrier(jnp.mean(grad * normed, axis=-1, keepdims=True))
    return recip * (grad - first - normed * second)

def reference(slab, pair, pair_mask, w_qkvg, w_out, w_bias, d_out):
    hi = lax.Precision.HIGHEST
    scale = 1.0 / DH ** 0.5
    normed_slab, slab_r = norm_stats(slab)
    x_slab = normed_slab.astype(jnp.bfloat16)
    flat_slab = x_slab.reshape(SLAB * N, C)
    proj = jnp.dot(flat_slab, w_qkvg.reshape(C, 4 * HD), preferred_element_type=jnp.float32).reshape(SLAB, N, 4, H, DH)
    queries = proj[:, :, 0].astype(jnp.bfloat16)
    keys_all = proj[:, :, 1].astype(jnp.bfloat16)
    values = proj[:, :, 2].astype(jnp.bfloat16)
    gate = jax.nn.sigmoid(proj[:, :, 3])
    normed_pair, pair_r = norm_stats(pair)
    x_pair = normed_pair.astype(jnp.bfloat16)
    bias = jnp.dot(x_pair.reshape(N * N, C), w_bias, preferred_element_type=jnp.float32).astype(jnp.bfloat16)
    bias = jnp.transpose(bias.reshape(N, N, H), (2, 0, 1)).astype(jnp.float32)
    d_o = jnp.dot(d_out.reshape(SLAB * N, C), jnp.transpose(w_out), preferred_element_type=jnp.float32).reshape(SLAB, N, H, DH)
    d_att = (d_o * gate).astype(jnp.bfloat16)
    keep_all = pair_mask == 1

    def one_row(d_bias, inputs):
        query_row, key_row, value_row, datt_row, keep_row = inputs
        qf = query_row.astype(jnp.float32)
        kf = key_row.astype(jnp.float32)
        vf = value_row.astype(jnp.float32)
        df = datt_row.astype(jnp.float32)
        raw = jnp.einsum('jhd,khd->hjk', qf, kf, precision=hi) * scale + bias
        logits = jnp.where(keep_row[None, None, :], raw, -1000000000.0)
        top = lax.optimization_barrier(jnp.max(logits, axis=-1, keepdims=True))
        expo = jnp.exp(logits - top)
        probs = expo / lax.optimization_barrier(jnp.sum(expo, axis=-1, keepdims=True))
        probs_b = probs.astype(jnp.bfloat16).astype(jnp.float32)
        attended = jnp.einsum('hjk,khd->jhd', probs_b, vf, precision=hi)
        d_probs = jnp.einsum('jhd,khd->hjk', df, vf, precision=hi)
        d_logits = probs * (d_probs - lax.optimization_barrier(jnp.sum(probs * d_probs, axis=-1, keepdims=True)))
        d_logits = jnp.where(keep_row[None, None, :], d_logits, 0.0)
        dl_b = d_logits.astype(jnp.bfloat16).astype(jnp.float32)
        d_query = (jnp.einsum('hjk,khd->jhd', dl_b, kf, precision=hi) * scale).astype(jnp.bfloat16)
        d_key = (jnp.einsum('hjk,jhd->khd', dl_b, qf, precision=hi) * scale).astype(jnp.bfloat16)
        d_value = jnp.einsum('hjk,jhd->khd', probs_b, df, precision=hi).astype(jnp.bfloat16)
        return (d_bias + d_logits, (attended, d_query, d_key, d_value))
    zero_bias = jnp.zeros((H, N, N), jnp.float32)
    d_bias, stacked = lax.scan(one_row, zero_bias, (queries, keys_all, values, d_att, keep_all))
    attended, d_queries, d_keys, d_values = stacked
    gated = (gate * attended).astype(jnp.bfloat16)
    d_gate = (d_o * attended * gate * (1.0 - gate)).astype(jnp.bfloat16)
    grads = jnp.stack([d_queries, d_keys, d_values, d_gate], axis=2).reshape(SLAB * N, 4 * HD)
    d_wqkvg = jnp.dot(jnp.transpose(flat_slab), grads, preferred_element_type=jnp.float32).reshape(C, 4, HD)
    d_wout = jnp.dot(jnp.transpose(gated.reshape(SLAB * N, HD)), d_out.reshape(SLAB * N, C), preferred_element_type=jnp.float32)
    d_xslab = jnp.dot(grads, jnp.transpose(w_qkvg.reshape(C, 4 * HD)), preferred_element_type=jnp.float32).reshape(SLAB, N, C)
    d_slab = norm_back(normed_slab, slab_r, d_xslab).astype(jnp.bfloat16)
    d_xpair = jnp.einsum('hjk,ch->jkc', d_bias, w_bias.astype(jnp.float32), precision=hi)
    d_pair = norm_back(normed_pair, pair_r, d_xpair).astype(jnp.bfloat16)
    d_wbias = jnp.einsum('jkc,hjk->ch', x_pair.astype(jnp.float32), d_bias, precision=hi)
    return (d_slab, d_pair, d_wqkvg, d_wout, d_wbias)
```

```python
import jax
import jax.numpy as jnp
from jax import lax
from jax.experimental import pallas as pl
from jax.experimental.pallas import tpu as pltpu
from jax.sharding import PartitionSpec as P

MESH = pl.DeviceIdType.MESH
F32 = jnp.float32
BF16 = jnp.bfloat16
N = 1024
C = 128
DH = 32
ROWS = 4
OWN = 16
BLK = 256
EPS = 1e-05
SCALE = 1.0 / DH**0.5


def nn(a, b):
    return lax.dot_general(a, b, (((1,), (0,)), ((), ())), preferred_element_type=F32)


def nt(a, b):
    return lax.dot_general(a, b, (((1,), (1,)), ((), ())), preferred_element_type=F32)


def norm_cols(t):
    cen = t - jnp.mean(t, axis=0, keepdims=True)
    r = lax.rsqrt(jnp.mean(cen * cen, axis=0, keepdims=True) + EPS)
    return cen * r, r


class Sems:
    def __init__(self):
        self.count = 0

    def take(self, n):
        first = self.count
        self.count += n
        return first


SEMS = Sems()
G1 = SEMS.take(1)
G2A = SEMS.take(4)
G2B = SEMS.take(4)
G3A = SEMS.take(4)
G3B = SEMS.take(4)
G4A = SEMS.take(4)
G4B = SEMS.take(4)
R1 = SEMS.take(4)
R2A = SEMS.take(4)
R2B = SEMS.take(4)
R3A = SEMS.take(4)
R3B = SEMS.take(4)
R4 = SEMS.take(1)
R5 = SEMS.take(4)
DXR = SEMS.take(16)
DXA = SEMS.take(16)
W1 = SEMS.take(1)
W2 = SEMS.take(4)
W3 = SEMS.take(4)
W4 = SEMS.take(1)
W5 = SEMS.take(1)
B1 = SEMS.take(1)
B2 = SEMS.take(4)
B3 = SEMS.take(4)
B4 = SEMS.take(1)


def kernel(
    slab, pair, mask, wt, wn, wout, wb, wq, wbar, dout,
    o_dslab, o_dpair, o_w, o_wb,
    plane, dbias, xpt, braw, yq, rp, own_bias, ys, rs, xst, zt, z, rhs, natt,
    dkv, gate_s, do_s, s1, r1, s2, r2a, r2b, s3, r3a, r3b, s4, r4, dbown, dbh, dball,
    dxs, dxr, dsl, wacc, w1r, wh, w2r, w3r, w4r, w5r, bsum, b1r, b2r, b3r, b4r,
    send, recv,
):
    r = lax.axis_index("rows")
    h = lax.axis_index("heads")
    c = lax.rem(r, 2)
    x = lax.rem(r // 2, 4)
    zh = lax.rem(r // 8, 2)
    y = r // 16

    def rid(y_, zh_, x_, c_):
        return ((y_ * 2 + zh_) * 4 + x_) * 2 + c_

    def off(a, d):
        return lax.rem(a + d, 4)

    core_peer = (rid(y, zh, x, 1 - c), h)
    zh_peer = (rid(y, 1 - zh, x, c), h)

    def x_peer(d):
        return (rid(y, zh, off(x, d), c), h)

    def y_peer(d):
        return (rid(off(y, d), zh, x, c), h)

    def h_peer(d):
        return (r, off(h, d))

    def copy(src, dst, sem, peer):
        return pltpu.make_async_remote_copy(
            src_ref=src, dst_ref=dst, send_sem=send.at[sem], recv_sem=recv.at[sem],
            device_id=peer, device_id_type=MESH,
        )

    barrier = pltpu.get_barrier_semaphore()
    peers = [core_peer, zh_peer]
    for d in (1, 2, 3):
        peers += [x_peer(d), y_peer(d), h_peer(d)]
    for peer in peers:
        pl.semaphore_signal(barrier, inc=1, device_id=peer, device_id_type=MESH)

    eye = (
        lax.broadcasted_iota(jnp.int32, (C, C), 0) == lax.broadcasted_iota(jnp.int32, (C, C), 1)
    ).astype(F32).astype(BF16)

    def pair_row(j, _):
        yt, rj = norm_cols(nt(eye, pair[j]))
        xb = yt.astype(BF16)
        xpt[j] = xb
        rp[pl.ds(j, 1), :] = rj
        ys[0] = yt
        yq[j] = ys[0, pl.ds(pl.multiple_of(h * DH, DH), DH), :]
        raw = nn(wb[...], xb)
        braw[j] = raw
        own_bias[pl.ds(j, 1), :] = raw[0:1, :]
        return 0

    lax.fori_loop(0, OWN, pair_row, 0)
    plane[y, zh, x, c] = own_bias[...].astype(BF16)
    pl.semaphore_wait(barrier, len(peers))

    g1 = copy(plane.at[y, zh, x, c], plane.at[y, zh, x, c], G1, zh_peer)
    g1.start()

    def slab_row(i, _):
        yt, ri = norm_cols(nt(eye, slab[i]))
        ys[i] = yt
        rs[pl.ds(i, 1), :] = ri
        xb = yt.astype(BF16)
        xst[i] = xb
        proj = nn(wt[...], xb)
        gate = 1.0 / (1.0 + jnp.exp(-proj[96:128]))
        do = nt(wout[...], dout[i])
        gate_s[i] = gate
        do_s[i] = do
        stack = jnp.concatenate([proj[0:96], do * gate], axis=0)
        zt[i] = stack.astype(BF16)
        z[i] = stack.T.astype(BF16)
        return 0

    g1.wait()
    g2 = []
    for d in (1, 2, 3):
        a = copy(plane.at[y, 0, x, c], plane.at[y, 0, x, c], G2A + d, x_peer(d))
        b = copy(plane.at[y, 1, x, c], plane.at[y, 1, x, c], G2B + d, y_peer(d))
        a.start()
        b.start()
        g2 += [a, b]
    lax.fori_loop(0, ROWS, slab_row, 0)
    wacc[...] = jnp.zeros(wacc.shape, F32)
    dball[...] = jnp.zeros(dball.shape, F32)
    rhs[...] = jnp.zeros(rhs.shape, BF16)
    for g in g2:
        g.wait()
    g3 = []
    for d in (1, 2, 3):
        a = copy(plane.at[y, 0, :, c], plane.at[y, 0, :, c], G3A + d, y_peer(d))
        b = copy(plane.at[:, 1, x, c], plane.at[:, 1, x, c], G3B + d, x_peer(d))
        a.start()
        b.start()
        g3 += [a, b]
    g4 = []

    def to_core(d):
        ya, xa = off(y + 4, -d), off(x + 4, -d)
        a = copy(plane.at[ya, 0, :, c], plane.at[ya, 0, :, c], G4A + d, core_peer)
        b = copy(plane.at[:, 1, xa, c], plane.at[:, 1, xa, c], G4B + d, core_peer)
        a.start()
        b.start()
        g4.extend([a, b])

    to_core(0)
    for d in (1, 2, 3):
        g3[2 * d - 2].wait_recv()
        g3[2 * d - 1].wait_recv()
        to_core(d)
    for g in g3:
        g.wait_send()
    for g in g4:
        g.wait()

    def r1_copy(yy):
        return copy(s1.at[yy], r1.at[yy], R1 + yy, core_peer)

    def block(i, keep, jb):
        rows = pl.ds(pl.multiple_of(jb * BLK, BLK), BLK)
        zj = z[i, rows, :]
        bias = plane[jb].reshape(BLK, N).astype(F32)
        logits = nn(zj, rhs[:, 0:N]) * SCALE + bias
        logits = jnp.where(keep, logits, -1e9)
        expo = jnp.exp(logits - jnp.max(logits, axis=1, keepdims=True))
        probs = expo * (1.0 / jnp.sum(expo, axis=1, keepdims=True))
        pb = probs.astype(BF16)
        dp = nn(zj, rhs[:, N : 2 * N])
        dl = probs * (dp - jnp.sum(probs * dp, axis=1, keepdims=True))
        dl = jnp.where(keep, dl, 0.0)
        dlb = dl.astype(BF16)
        dl6 = dl.reshape(2, 4, 2, OWN, N)

        @pl.when(i == 0)
        def _():
            dbias[jb] = dl6

        @pl.when(i > 0)
        def _():
            dbias[jb] += dl6

        zall = z[i]
        lane = lax.broadcasted_iota(jnp.int32, (BLK, C), 1)
        natt[rows, :] = jnp.where(lane < 64, nn(dlb, zall), nn(pb, zall))
        dkv[0:DH, :] += nn(zt[i, 0:DH, rows], dlb)
        dkv[DH:64, :] += nn(zt[i, 96:128, rows], pb)

        @pl.when(i == ROWS - 1)
        def _():
            s1[jb] = dbias[jb, :, :, 1 - c].astype(BF16)
            r1_copy(jb).start()

    def dx_copies(i):
        return [
            copy(dxs.at[i, off(h, d)], dxr.at[i, d], DXR + 4 * i + d, h_peer(d))
            for d in (1, 2, 3)
        ]

    def slab_copies(i):
        return [copy(dsl.at[i, h], dsl.at[i, h], DXA + 4 * i + d, h_peer(d)) for d in (1, 2, 3)]

    def finish_slab(i):
        for cp in dx_copies(i):
            cp.wait()
        g = dxs[i, h].astype(F32)
        for d in (1, 2, 3):
            g = g + dxr[i, d].astype(F32)
        cols = pl.ds(pl.multiple_of(h * BLK, BLK), BLK)
        yt = ys[i, :, cols]
        ri = rs[pl.ds(i, 1), cols]
        out = ri * (
            g - jnp.mean(g, axis=0, keepdims=True) - yt * jnp.mean(g * yt, axis=0, keepdims=True)
        )
        dsl[i, h] = out.T.astype(BF16)
        for cp in slab_copies(i):
            cp.start()

    def attend(i, _):
        keep = mask[pl.ds(i, 1), :] == 1
        rhs[0:DH, 0:N] = zt[i, 32:64, :]
        rhs[96:128, N : 2 * N] = zt[i, 64:96, :]
        dkv[...] = jnp.zeros(dkv.shape, F32)

        def step(jb, _):
            block(i, keep, jb)
            return 0

        lax.fori_loop(0, N // BLK, step, 0)
        nat = natt[...].T
        gate = gate_s[i]
        do = do_s[i]
        att = nat[64:96]
        gated = (gate * att).astype(BF16)
        dgate = do * att * gate * (1.0 - gate)
        grads = jnp.concatenate(
            [nat[32:64] * SCALE, dkv[0:DH, :] * SCALE, dkv[DH:64, :], dgate], axis=0
        ).astype(BF16)
        wacc[0:C, :] += nt(xst[i], grads)
        wacc[C : C + DH, :] += nn(gated, dout[i])
        dx = nn(wn[...], grads).astype(BF16)
        for q in range(4):
            dxs[i, q] = dx[:, q * BLK : (q + 1) * BLK]
        for cp in dx_copies(i):
            cp.start()

        @pl.when(i > 0)
        def _():
            finish_slab(i - 1)

        return 0

    lax.fori_loop(0, ROWS, attend, 0)

    half = pl.ds(pl.multiple_of(c * 80, 80), 80)
    other = pl.ds(pl.multiple_of((1 - c) * 80, 80), 80)
    w1 = copy(wacc.at[other], w1r, W1, core_peer)
    w1.start()
    r2 = []

    def r1_sum(yy):
        cp = r1_copy(yy)
        cp.wait()
        total = dbias[yy, :, :, c] + r1[yy].astype(F32)
        dbias[yy, :, :, c] = total
        s2[yy] = total.astype(BF16)

    for d in (1, 2, 3):
        r1_sum(off(y, d))
        a = copy(s2.at[off(y, d), 0], r2a.at[d], R2A + d, y_peer(d))
        a.start()
        r2.append(a)
    r1_sum(y)
    for d in (1, 2, 3):
        b = copy(s2.at[:, 1, off(x, d)], r2b.at[d], R2B + d, x_peer(d))
        b.start()
        r2.append(b)
    finish_slab(ROWS - 1)
    w1.wait()
    wh[0] = wacc[half, :] + w1r[...]
    w2 = [copy(wh.at[0], w2r.at[d], W2 + d, x_peer(d)) for d in (1, 2, 3)]
    for cp in w2:
        cp.start()
    for cp in r2:
        cp.wait()
    t0 = dbias[y, 0, :, c]
    t1 = dbias[:, 1, x, c]
    for d in (1, 2, 3):
        t0 = t0 + r2a[d].astype(F32)
        t1 = t1 + r2b[d].astype(F32)
    s3[0] = t0
    s3[1] = t1
    r3 = []
    for d in (1, 2, 3):
        a = copy(s3.at[0, off(x, d)], r3a.at[d], R3A + d, x_peer(d))
        b = copy(s3.at[1, off(y, d)], r3b.at[d], R3B + d, y_peer(d))
        a.start()
        b.start()
        r3 += [a, b]
    for cp in w2:
        cp.wait()
    wh[1] = wh[0] + w2r[1] + w2r[2] + w2r[3]
    w3 = [copy(wh.at[1], w3r.at[d], W3 + d, y_peer(d)) for d in (1, 2, 3)]
    for cp in w3:
        cp.start()
    for cp in r3:
        cp.wait()
    s4[0] = s3[0, x] + r3a[1] + r3a[2] + r3a[3]
    s4[1] = s3[1, y] + r3b[1] + r3b[2] + r3b[3]
    cp4 = copy(s4.at[1 - zh], r4, R4, zh_peer)
    cp4.start()
    for cp in w3:
        cp.wait()
    wh[2] = wh[1] + w3r[1] + w3r[2] + w3r[3]
    w4 = copy(wh.at[2], w4r, W4, zh_peer)
    w4.start()
    cp4.wait()
    db = s4[zh] + r4[...]
    dbb = db.astype(BF16)
    dbown[...] = dbb
    r5 = [copy(dbown, dbh.at[d], R5 + d, h_peer(d)) for d in (1, 2, 3)]
    for cp in r5:
        cp.start()

    own_bias[...] = db
    bsum[0] = jnp.zeros((OWN, C), F32)
    row_of = lax.broadcasted_iota(jnp.int32, (OWN, N), 0)

    def wb_row(j, _):
        picked = jnp.where(row_of == j, own_bias[...], 0.0)
        hi = picked.astype(BF16)
        lo = (picked - hi.astype(F32)).astype(BF16)
        bsum[0] += nt(hi, xpt[j]) + nt(lo, xpt[j])
        return 0

    lax.fori_loop(0, OWN, wb_row, 0)
    b1 = copy(bsum.at[0], b1r, B1, core_peer)
    b1.start()
    w4.wait()
    wh[3] = wh[2] + w4r[...]
    w5 = copy(wh.at[3], w5r, W5, core_peer)
    w5.start()
    b1.wait()
    bsum[1] = bsum[0] + b1r[...]
    b2 = [copy(bsum.at[1], b2r.at[d], B2 + d, x_peer(d)) for d in (1, 2, 3)]
    for cp in b2:
        cp.start()

    for cp in r5:
        cp.wait()
    dball[:, 0, :] = dbb.astype(F32)
    for d in (1, 2, 3):
        dball[:, d, :] = dbh[d].astype(F32)

    def dpair_row(j, _):
        dbj = dball[j]
        g = nn(wq[...], dbj.astype(BF16))
        first = jnp.sum(dbj * wbar[:, 0:1], axis=0, keepdims=True)
        second = jnp.sum(dbj * braw[j], axis=0, keepdims=True) * (1.0 / C)
        o_dpair[j] = (rp[pl.ds(j, 1), :] * (g - first - yq[j] * second)).astype(BF16)
        return 0

    lax.fori_loop(0, 8, dpair_row, 0)
    for cp in b2:
        cp.wait()
    bsum[2] = bsum[1] + b2r[1] + b2r[2] + b2r[3]
    b3 = [copy(bsum.at[2], b3r.at[d], B3 + d, y_peer(d)) for d in (1, 2, 3)]
    for cp in b3:
        cp.start()
    lax.fori_loop(8, OWN, dpair_row, 0)
    for cp in b3:
        cp.wait()
    bsum[3] = bsum[2] + b3r[1] + b3r[2] + b3r[3]
    b4 = copy(bsum.at[3], b4r, B4, zh_peer)
    b4.start()

    def slab_wait(i, _):
        for cp in slab_copies(i):
            cp.wait()
        return 0

    lax.fori_loop(0, ROWS, slab_wait, 0)
    for i in range(ROWS):
        for q in range(4):
            o_dslab[i, q * BLK : (q + 1) * BLK, :] = dsl[i, q]
    w5.wait()
    o_w[half, :] = wh[3]
    o_w[other, :] = w5r[...]
    b4.wait()
    o_wb[...] = bsum[3] + b4r[...]


def scratch():
    v = pltpu.VMEM
    return [
        v((4, 2, 4, 2, OWN, N), BF16),
        v((4, 2, 4, 2, OWN, N), F32),
        v((OWN, C, N), BF16),
        v((OWN, OWN, N), F32),
        v((OWN, DH, N), F32),
        v((OWN, N), F32),
        v((OWN, N), F32),
        v((ROWS, C, N), F32),
        v((8, N), F32),
        v((ROWS, C, N), BF16),
        v((ROWS, C, N), BF16),
        v((ROWS, N, C), BF16),
        v((C, 2 * N), BF16),
        v((N, C), F32),
        v((64, N), F32),
        v((ROWS, DH, N), F32),
        v((ROWS, DH, N), F32),
        v((4, 2, 4, OWN, N), BF16),
        v((4, 2, 4, OWN, N), BF16),
        v((4, 2, 4, OWN, N), BF16),
        v((4, 4, OWN, N), BF16),
        v((4, 4, OWN, N), BF16),
        v((2, 4, OWN, N), F32),
        v((4, OWN, N), F32),
        v((4, OWN, N), F32),
        v((2, OWN, N), F32),
        v((OWN, N), F32),
        v((OWN, N), BF16),
        v((4, OWN, N), BF16),
        v((OWN, OWN, N), F32),
        v((ROWS, 4, C, BLK), BF16),
        v((ROWS, 4, C, BLK), BF16),
        v((ROWS, 4, BLK, C), BF16),
        v((C + DH, C), F32),
        v((80, C), F32),
        v((4, 80, C), F32),
        v((4, 80, C), F32),
        v((4, 80, C), F32),
        v((80, C), F32),
        v((80, C), F32),
        v((4, OWN, C), F32),
        v((OWN, C), F32),
        v((4, OWN, C), F32),
        v((4, OWN, C), F32),
        v((OWN, C), F32),
        pltpu.SemaphoreType.DMA((SEMS.count,)),
        pltpu.SemaphoreType.DMA((SEMS.count,)),
    ]


def shards(slab, pair, pair_mask, w_qkvg, w_out, w_bias, d_out):
    head = lax.axis_index("heads")
    wn = w_qkvg.reshape(C, C)
    wt = wn.T
    order = lax.rem(head + 4 - jnp.arange(4), 4)
    wrel = jnp.take(w_bias, order, axis=1)
    wb = jnp.zeros((16, C), BF16).at[0:4].set(wrel.T)
    quarter = lax.dynamic_slice_in_dim(wrel, head * DH, DH, 0)
    wq = jnp.zeros((DH, 16), BF16).at[:, 0:4].set(quarter)
    mean = jnp.mean(wrel.astype(F32), axis=0)
    wbar = jnp.zeros((16, C), F32).at[0:4].set(jnp.broadcast_to(mean[:, None], (4, C)))
    vm = pl.BlockSpec(memory_space=pltpu.VMEM)
    d_slab, d_pair, w, wbg = pl.pallas_call(
        kernel,
        out_shape=(
            jax.ShapeDtypeStruct((ROWS, N, C), BF16),
            jax.ShapeDtypeStruct((OWN, DH, N), BF16),
            jax.ShapeDtypeStruct((C + DH, C), F32),
            jax.ShapeDtypeStruct((OWN, C), F32),
        ),
        in_specs=[vm] * 10,
        out_specs=(vm,) * 4,
        scratch_shapes=scratch(),
        compiler_params=pltpu.CompilerParams(
            collective_id=0, has_side_effects=True, vmem_limit_bytes=60 * 1024 * 1024
        ),
    )(slab, pair, pair_mask, wt, wn, w_out, wb, wq, wbar, d_out)
    return (
        d_slab,
        jnp.swapaxes(d_pair, 1, 2),
        w[0:C].reshape(C, 4, DH),
        w[C:],
        jnp.sum(wbg, axis=0)[:, None],
    )


def solution(mesh):
    placed = (
        P("rows", None, None),
        P("rows", None, None),
        P("rows", None),
        P(None, None, "heads"),
        P("heads", None),
        P(),
        P("rows", None, None),
    )
    return jax.shard_map(
        shards,
        mesh=mesh,
        in_specs=placed,
        out_specs=(
            P("rows", None, None),
            P("rows", None, "heads"),
            P(None, None, "heads"),
            P("heads", None),
            P(None, "heads"),
        ),
        check_vma=False,
    )
```

```python
import jax
import jax.numpy as jnp
from jax import lax
from jax.experimental import pallas as pl
from jax.experimental.pallas import tpu as pltpu
from jax.sharding import PartitionSpec as P

MESH = pl.DeviceIdType.MESH
F32 = jnp.float32
BF16 = jnp.bfloat16
N = 1024
C = 128
DH = 32
ROWS = 4
OWN = 16
BLK = 256
HALF = 512
EPS = 1e-05
SCALE = 1.0 / DH**0.5


def nn(a, b):
    return lax.dot_general(a, b, (((1,), (0,)), ((), ())), preferred_element_type=F32)


def nt(a, b):
    return lax.dot_general(a, b, (((1,), (1,)), ((), ())), preferred_element_type=F32)


def norm_cols(t):
    cen = t - jnp.mean(t, axis=0, keepdims=True)
    r = lax.rsqrt(jnp.mean(cen * cen, axis=0, keepdims=True) + EPS)
    return cen * r, r


class Sems:
    def __init__(self):
        self.count = 0

    def take(self, n):
        first = self.count
        self.count += n
        return first


SEMS = Sems()
G1 = SEMS.take(1)
GP = SEMS.take(32)
GC = SEMS.take(2)
R1 = SEMS.take(2)
R2 = SEMS.take(16)
R3 = SEMS.take(16)
R4 = SEMS.take(8)
DXR = SEMS.take(16)
DXA = SEMS.take(16)
W1 = SEMS.take(8)
W2 = SEMS.take(8)
W3 = SEMS.take(8)
B1 = SEMS.take(8)
B2 = SEMS.take(8)
LOW = slice(0, HALF)
HIGH = slice(HALF, N)


def kernel(
    slab_h, pair_h, mask, wt, wout, wbias, dout_h,
    o_dslab, o_dpair, o_dw, o_dwout, o_dwb,
    slab, pair, dout, wn, wbt, wb,
    plane, dbias, xpt, braw, yq, rp, own_bias, ys, rs, xst, zq, z, rhs, natt,
    dkv, gate_s, do_s, s1, r1, s2, r2a, r2b, s3, r3a, r3b, s4, r4, dball,
    dxs, dxr, dsl, wacc, w1r, wpart, w2r, wtot, fold, bsum, b1r, b2r,
    send, recv, load,
):
    r = lax.axis_index("rows")
    h = lax.axis_index("heads")
    c = lax.rem(r, 2)
    x = lax.rem(r // 2, 4)
    zh = lax.rem(r // 8, 2)
    y = r // 16
    oz = 1 - zh

    def off(a, d):
        return lax.rem(a + d, 4)

    def flip(a, e):
        return 1 - a if e else a

    def peer(dy=0, ez=0, dx=0, ec=0, dh=0):
        row = ((off(y, dy) * 2 + flip(zh, ez)) * 4 + off(x, dx)) * 2 + flip(c, ec)
        return (row, off(h, dh))

    def copy(src, dst, sem, to):
        return pltpu.make_async_remote_copy(
            src_ref=src, dst_ref=dst, send_sem=send.at[sem], recv_sem=recv.at[sem],
            device_id=to, device_id_type=MESH,
        )

    loads = [pltpu.make_async_copy(pair_h.at[4 * k : 4 * k + 4], pair.at[4 * k : 4 * k + 4], load.at[k]) for k in range(4)]
    loads.append(pltpu.make_async_copy(slab_h, slab, load.at[4]))
    loads.append(pltpu.make_async_copy(dout_h, dout, load.at[5]))
    for cp in loads:
        cp.start()

    near = [(dx, ec) for dx in range(4) for ec in range(2) if dx or ec]
    far = [(dy, ez) for dy in range(4) for ez in range(2) if dy or ez]
    peers = [peer(dx=a, ec=b) for a, b in near] + [peer(dy=a, ez=b) for a, b in far]
    for d in (1, 2, 3):
        peers += [peer(dh=d), peer(ez=1, dh=d)]
    barrier = pltpu.get_barrier_semaphore()
    for to in peers:
        pl.semaphore_signal(barrier, inc=1, device_id=to, device_id_type=MESH)

    eye = (
        lax.broadcasted_iota(jnp.int32, (C, C), 0) == lax.broadcasted_iota(jnp.int32, (C, C), 1)
    ).astype(F32).astype(BF16)

    wn[...] = nt(eye, wt[...]).astype(BF16)
    row16 = lax.broadcasted_iota(jnp.int32, (16, C), 0)
    heads = wbias[...].astype(F32)
    wrel = jnp.zeros((16, C), F32)
    for k in range(4):
        wrel = wrel + jnp.where(row16 == off(h + 4, -k), heads[k : k + 1, :], 0.0)
    wb[...] = wrel.astype(BF16)
    wbt[...] = nt(eye, wrel.astype(BF16))
    wbar = jnp.mean(wrel, axis=1, keepdims=True)

    def pair_row(j, _):
        yt, rj = norm_cols(nt(eye, pair[j]))
        xb = yt.astype(BF16)
        xpt[j] = xb
        rp[pl.ds(j, 1), :] = rj
        ys[lax.rem(j, 2)] = yt
        yq[j] = ys[lax.rem(j, 2), pl.ds(pl.multiple_of(h * DH, DH), DH), :]
        raw = nn(wb[...], xb)
        braw[j] = raw
        own_bias[pl.ds(j, 1), :] = raw[0:1, :]
        return 0

    for k in range(4):
        loads[k].wait()
        lax.fori_loop(4 * k, 4 * k + 4, pair_row, 0, unroll=True)
    plane[y, zh, x, c] = own_bias[...].astype(BF16)
    pl.semaphore_wait(barrier, len(peers))

    def gather_first(s):
        zs = flip(zh, s)
        out = []
        for d in (1, 2, 3):
            low = plane.at[y, zs, x, c, :, LOW]
            high = plane.at[y, zs, x, c, :, HIGH]
            out.append(copy(low, low, GP + 16 * s + d, peer(dx=d)))
            out.append(copy(high, high, GP + 16 * s + 4 + d, peer(dy=d)))
        return out

    def gather_second(s):
        zs = flip(zh, s)
        out = []
        for d in (1, 2, 3):
            low = plane.at[y, zs, :, c, :, LOW]
            high = plane.at[:, zs, x, c, :, HIGH]
            out.append(copy(low, low, GP + 16 * s + 8 + d, peer(dy=d)))
            out.append(copy(high, high, GP + 16 * s + 12 + d, peer(dx=d)))
        return out

    def gather_core(s):
        zs = flip(zh, s)
        return copy(plane.at[:, zs, :, c], plane.at[:, zs, :, c], GC + s, peer(ec=1))

    def begin(copies):
        for cp in copies:
            cp.start()

    def end(copies):
        for cp in copies:
            cp.wait()

    g1 = copy(plane.at[y, zh, x, c], plane.at[y, zh, x, c], G1, peer(ez=1))
    g1.start()
    ga1 = gather_first(0)
    begin(ga1)

    def slab_row(i, _):
        yt, ri = norm_cols(nt(eye, slab[i]))
        ys[i] = yt
        rs[pl.ds(i, 1), :] = ri
        xb = yt.astype(BF16)
        xst[i] = xb
        proj = nn(wt[...], xb)
        gate = 1.0 / (1.0 + jnp.exp(-proj[96:128]))
        do = nt(wout[...], dout[i])
        gate_s[i] = gate
        do_s[i] = do
        datt = do * gate
        stack = jnp.concatenate([proj[0:96], datt], axis=0)
        z[i] = stack.T.astype(BF16).reshape(4, 2, 128, C)
        both = jnp.concatenate([proj[0:DH], datt], axis=0).astype(BF16)
        for k in range(8):
            zq[i, k] = both[:, k * 128 : (k + 1) * 128]
        rhs[i, 0:DH, 0:N] = proj[32:64].astype(BF16)
        rhs[i, 96:128, N : 2 * N] = proj[64:96].astype(BF16)
        return 0

    rhs[...] = jnp.zeros(rhs.shape, BF16)
    loads[4].wait()
    loads[5].wait()
    lax.fori_loop(0, 2, slab_row, 0)
    end(ga1)
    ga2 = gather_second(0)
    begin(ga2)
    g1.wait()
    gb1 = gather_first(1)
    begin(gb1)
    lax.fori_loop(2, ROWS, slab_row, 0)
    wacc[...] = jnp.zeros(wacc.shape, F32)
    dkv[...] = jnp.zeros(dkv.shape, F32)
    dbias[...] = jnp.zeros(dbias.shape, F32)
    end(gb1)
    gb2 = gather_second(1)
    begin(gb2)
    end(ga2)
    gac = gather_core(0)
    gac.start()
    gac.wait()

    def block(i, yy, zs):
        keep = mask[pl.ds(i, 1), :] == 1
        two = pl.ds(2 * yy, 2)
        zj = z[i, two, zs].reshape(BLK, C)
        bias = plane[two, zs].reshape(BLK, N).astype(F32)
        logits = nn(zj, rhs[i, :, 0:N]) * SCALE + bias
        logits = jnp.where(keep, logits, -1e9)
        expo = jnp.exp(logits - jnp.max(logits, axis=1, keepdims=True))
        probs = expo * (1.0 / jnp.sum(expo, axis=1, keepdims=True))
        pb = probs.astype(BF16)
        dp = nn(zj, rhs[i, :, N : 2 * N])
        dl = probs * (dp - jnp.sum(probs * dp, axis=1, keepdims=True))
        dl = jnp.where(keep, dl, 0.0)
        dlb = dl.astype(BF16)
        dbias[two, zs] += dl.reshape(2, 4, 2, OWN, N)
        zall = z[i].reshape(N, C)
        lane = lax.broadcasted_iota(jnp.int32, (BLK, C), 1)
        nat = jnp.where(lane < 64, nn(dlb, zall), nn(pb, zall))
        natt[i, two, zs] = nat.reshape(2, 128, C)
        left = jnp.concatenate([zq[i, 4 * yy + zs], zq[i, 4 * yy + 2 + zs]], axis=1)
        dkv[i, 0:DH, :] += nn(left[0:DH], dlb)
        dkv[i, DH:64, :] += nn(left[DH:64], pb)

    def own_half(t, _):
        block(t // 2, lax.rem(t, 2), zh)
        return 0

    def other_half(t, _):
        block(t // 2, lax.rem(t, 2), oz)
        return 0

    def dx_copies(i):
        return [
            copy(dxs.at[i, off(h, d)], dxr.at[i, d], DXR + 4 * i + d, peer(dh=d))
            for d in (1, 2, 3)
        ]

    def slab_copies(i):
        return [copy(dsl.at[i, h], dsl.at[i, h], DXA + 4 * i + d, peer(dh=d)) for d in (1, 2, 3)]

    def finish_slab(i):
        end(dx_copies(i))
        g = dxs[i, h].astype(F32)
        for d in (1, 2, 3):
            g = g + dxr[i, d].astype(F32)
        cols = pl.ds(pl.multiple_of(h * BLK, BLK), BLK)
        yt = ys[i, :, cols]
        ri = rs[pl.ds(i, 1), cols]
        out = ri * (
            g - jnp.mean(g, axis=0, keepdims=True) - yt * jnp.mean(g * yt, axis=0, keepdims=True)
        )
        dsl[i, h] = out.T.astype(BF16)
        begin(slab_copies(i))

    def finish_row(i):
        nat = natt[i].reshape(N, C).T
        gate = gate_s[i]
        do = do_s[i]
        att = nat[64:96]
        gated = (gate * att).astype(BF16)
        dgate = do * att * gate * (1.0 - gate)
        grads = jnp.concatenate(
            [nat[32:64] * SCALE, dkv[i, 0:DH, :] * SCALE, dkv[i, DH:64, :], dgate], axis=0
        ).astype(BF16)
        dx = nn(wn[...], grads).astype(BF16)
        for q in range(4):
            dxs[i, q] = dx[:, q * BLK : (q + 1) * BLK]
        begin(dx_copies(i))
        wacc[0:C, :] += nt(grads, xst[i])
        wacc[C : C + DH, :] += nn(gated, dout[i])

    def sum_core(s):
        zs = flip(zh, s)
        s1[s] = dbias[:, zs, :, 1 - c].astype(BF16)
        return copy(s1.at[s], r1.at[s], R1 + s, peer(ec=1))

    def sum_first(s):
        zs = flip(zh, s)
        for yy in range(4):
            total = dbias[yy, zs, :, c] + r1[s, yy].astype(F32)
            dbias[yy, zs, :, c] = total
            s2[s, yy] = total.astype(BF16)
        out = []
        for d in (1, 2, 3):
            low = s2.at[s, off(y, d), :, :, LOW]
            high = s2.at[s, :, off(x, d), :, HIGH]
            out.append(copy(low, r2a.at[s, d], R2 + 8 * s + d, peer(dy=d)))
            out.append(copy(high, r2b.at[s, d], R2 + 8 * s + 4 + d, peer(dx=d)))
        return out

    def sum_second(s):
        zs = flip(zh, s)
        low = dbias[y, zs, :, c, :, LOW]
        high = dbias[:, zs, x, c, :, HIGH]
        for d in (1, 2, 3):
            low = low + r2a[s, d].astype(F32)
            high = high + r2b[s, d].astype(F32)
        s3[s, 0] = low.astype(BF16)
        s3[s, 1] = high.astype(BF16)
        dbias[y, zs, :, c, :, LOW] = low
        dbias[:, zs, x, c, :, HIGH] = high
        out = []
        for d in (1, 2, 3):
            out.append(copy(s3.at[s, 0, off(x, d)], r3a.at[s, d], R3 + 8 * s + d, peer(dx=d)))
            out.append(copy(s3.at[s, 1, off(y, d)], r3b.at[s, d], R3 + 8 * s + 4 + d, peer(dy=d)))
        return out

    def sum_last(s):
        zs = flip(zh, s)
        low = dbias[y, zs, x, c, :, LOW]
        high = dbias[y, zs, x, c, :, HIGH]
        for d in (1, 2, 3):
            low = low + r3a[s, d].astype(F32)
            high = high + r3b[s, d].astype(F32)
        both = jnp.concatenate([low, high], axis=1)
        s4[s] = both.astype(BF16)
        out = []
        for d in range(4):
            if s or d:
                out.append(copy(s4.at[s], r4.at[s, d], R4 + 4 * s + d, peer(ez=s, dh=d)))
        return both, out

    lax.fori_loop(0, 4, own_half, 0)
    end(gb2)
    gbc = gather_core(1)
    gbc.start()
    lax.fori_loop(4, 8, own_half, 0)
    ra1 = sum_core(0)
    ra1.start()
    gbc.wait()
    lax.fori_loop(0, 2, other_half, 0)
    finish_row(0)
    ra1.wait()
    ra2 = sum_first(0)
    begin(ra2)
    lax.fori_loop(2, 4, other_half, 0)
    finish_row(1)
    lax.fori_loop(4, 6, other_half, 0)
    finish_row(2)
    end(ra2)
    ra3 = sum_second(0)
    begin(ra3)
    lax.fori_loop(6, 8, other_half, 0)
    rb1 = sum_core(1)
    rb1.start()
    finish_row(3)
    chunk = 24

    def wslice(k):
        return pl.ds(pl.multiple_of(k * chunk, 8), chunk)

    def wid(dx, ec):
        return off(x, dx) * 2 + flip(c, ec)

    w1 = [
        copy(wacc.at[wslice(wid(a, b))], w1r.at[2 * a + b], W1 + 2 * a + b, peer(dx=a, ec=b))
        for a, b in near
    ]
    rb1.wait()
    rb2 = sum_first(1)
    begin(rb2)
    begin(w1)
    finish_slab(0)
    end(ra3)
    own, ra4 = sum_last(0)
    own_bias[...] = own
    begin(ra4)
    end(w1)
    part = wacc[wslice(wid(0, 0)), :]
    for a, b in near:
        part = part + w1r[2 * a + b]
    wpart[...] = part
    w2 = [copy(wpart, w2r.at[2 * a + b], W2 + 2 * a + b, peer(dy=a, ez=b)) for a, b in far]
    begin(w2)
    end(rb2)
    rb3 = sum_second(1)
    begin(rb3)
    finish_slab(1)
    end(rb3)
    _, rb4 = sum_last(1)
    begin(rb4)
    end(w2)
    part = wpart[...]
    for a, b in far:
        part = part + w2r[2 * a + b]
    wtot[wslice(wid(0, 0)), :] = part
    w3 = [
        copy(
            wtot.at[wslice(wid(0, 0))], wtot.at[wslice(wid(0, 0))], W3 + 2 * a + b,
            peer(dx=a, ec=b),
        )
        for a, b in near
    ]
    begin(w3)
    finish_slab(2)
    end(ra4)
    end(rb4)

    db = own_bias[...] + r4[1, 0].astype(F32)
    own_bias[...] = db
    dball[:, 0, :] = db
    for d in (1, 2, 3):
        dball[:, d, :] = r4[0, d].astype(F32) + r4[1, d].astype(F32)
    dball[:, 4:16, :] = jnp.zeros((OWN, 12, N), F32)

    def wb_part(k, _):
        sub = pl.ds(pl.multiple_of(k * 32, 32), 32)
        acc = xpt[0, sub, :].astype(F32) * own_bias[0:1, :]
        for j in range(1, OWN):
            acc = acc + xpt[j, sub, :].astype(F32) * own_bias[j : j + 1, :]
        total = acc[:, 0:128]
        for q in range(1, 8):
            total = total + acc[:, q * 128 : (q + 1) * 128]
        fold[sub, :] = total
        return 0

    lax.fori_loop(0, 4, wb_part, 0)
    total = fold[...]
    hi = total.astype(BF16)
    mid = (total - hi.astype(F32)).astype(BF16)
    lo = (total - hi.astype(F32) - mid.astype(F32)).astype(BF16)
    ones = jnp.ones((16, C), F32).astype(BF16)
    bsum[0] = (nt(ones, hi) + nt(ones, mid) + nt(ones, lo))[0:8]
    b1 = [copy(bsum.at[0], b1r.at[2 * a + b], B1 + 2 * a + b, peer(dx=a, ec=b)) for a, b in near]
    begin(b1)

    def dpair_row(j, _):
        dbj = dball[j]
        wq = wbt[pl.ds(pl.multiple_of(h * DH, DH), DH), :].astype(BF16)
        g = nn(wq, dbj.astype(BF16))
        first = jnp.sum(dbj * wbar, axis=0, keepdims=True)
        second = jnp.sum(dbj * braw[j], axis=0, keepdims=True) * (1.0 / C)
        o_dpair[j] = (rp[pl.ds(j, 1), :] * (g - first - yq[j] * second)).astype(BF16)
        return 0

    finish_slab(3)
    lax.fori_loop(0, 8, dpair_row, 0, unroll=4)
    end(b1)
    part = bsum[0]
    for a, b in near:
        part = part + b1r[2 * a + b]
    bsum[1] = part
    b2 = [copy(bsum.at[1], b2r.at[2 * a + b], B2 + 2 * a + b, peer(dy=a, ez=b)) for a, b in far]
    begin(b2)
    lax.fori_loop(8, OWN, dpair_row, 0, unroll=4)
    end(w3)
    o_dw[...] = wtot[0:C, :]
    o_dwout[...] = wtot[C : C + DH, :]
    for i in range(ROWS):
        end(slab_copies(i))
        for q in range(4):
            o_dslab[i, q * BLK : (q + 1) * BLK, :] = dsl[i, q]
    end(b2)
    part = bsum[1]
    for a, b in far:
        part = part + b2r[2 * a + b]
    o_dwb[...] = part[0:1, :]


def scratch():
    v = pltpu.VMEM
    return [
        v((ROWS, N, C), BF16),
        v((OWN, N, C), BF16),
        v((ROWS, N, C), BF16),
        v((C, C), BF16),
        v((C, 16), F32),
        v((16, C), BF16),
        v((4, 2, 4, 2, OWN, N), BF16),
        v((4, 2, 4, 2, OWN, N), F32),
        v((OWN, C, N), BF16),
        v((OWN, OWN, N), F32),
        v((OWN, DH, N), F32),
        v((OWN, N), F32),
        v((OWN, N), F32),
        v((ROWS, C, N), F32),
        v((8, N), F32),
        v((ROWS, C, N), BF16),
        v((ROWS, 8, 64, 128), BF16),
        v((ROWS, 4, 2, 128, C), BF16),
        v((ROWS, C, 2 * N), BF16),
        v((ROWS, 4, 2, 128, C), F32),
        v((ROWS, 64, N), F32),
        v((ROWS, DH, N), F32),
        v((ROWS, DH, N), F32),
        v((2, 4, 4, OWN, N), BF16),
        v((2, 4, 4, OWN, N), BF16),
        v((2, 4, 4, OWN, N), BF16),
        v((2, 4, 4, OWN, HALF), BF16),
        v((2, 4, 4, OWN, HALF), BF16),
        v((2, 2, 4, OWN, HALF), BF16),
        v((2, 4, OWN, HALF), BF16),
        v((2, 4, OWN, HALF), BF16),
        v((2, OWN, N), BF16),
        v((2, 4, OWN, N), BF16),
        v((OWN, OWN, N), F32),
        v((ROWS, 4, C, BLK), BF16),
        v((ROWS, 4, C, BLK), BF16),
        v((ROWS, 4, BLK, C), BF16),
        v((192, C), F32),
        v((8, 24, C), F32),
        v((24, C), F32),
        v((8, 24, C), F32),
        v((192, C), F32),
        v((C, C), F32),
        v((2, 8, C), F32),
        v((8, 8, C), F32),
        v((8, 8, C), F32),
        pltpu.SemaphoreType.DMA((SEMS.count,)),
        pltpu.SemaphoreType.DMA((SEMS.count,)),
        pltpu.SemaphoreType.DMA((6,)),
    ]


def hand_on(*refs):
    n = len(refs) // 2
    copies = [pltpu.make_async_copy(refs[k], refs[n + k], refs[-1].at[k]) for k in range(n)]
    for cp in copies:
        cp.start()
    for cp in copies:
        cp.wait()


def shards(slab, pair, pair_mask, w_qkvg, w_out, w_bias, d_out):
    wt = jnp.transpose(w_qkvg, (1, 2, 0)).reshape(C, C)
    vm = pl.BlockSpec(memory_space=pltpu.VMEM)
    anywhere = pl.BlockSpec(memory_space=pl.ANY)
    shapes = (
        jax.ShapeDtypeStruct((ROWS, N, C), BF16),
        jax.ShapeDtypeStruct((OWN, DH, N), BF16),
        jax.ShapeDtypeStruct((C, C), F32),
        jax.ShapeDtypeStruct((DH, C), F32),
        jax.ShapeDtypeStruct((1, C), F32),
    )
    outs = pl.pallas_call(
        kernel,
        out_shape=shapes,
        in_specs=[anywhere, anywhere, vm, vm, vm, vm, anywhere],
        out_specs=(vm,) * 5,
        scratch_shapes=scratch(),
        compiler_params=pltpu.CompilerParams(
            collective_id=0, has_side_effects=True, vmem_limit_bytes=60 * 1024 * 1024
        ),
    )(slab, pair, pair_mask, wt, w_out, w_bias.T, d_out)
    d_slab, d_pair, dw, dwout, dwb = pl.pallas_call(
        hand_on,
        out_shape=shapes,
        in_specs=[pl.BlockSpec(memory_space=pltpu.HBM)] * 5,
        out_specs=(anywhere,) * 5,
        scratch_shapes=[pltpu.SemaphoreType.DMA((5,))],
    )(*outs)
    return (
        d_slab,
        jnp.swapaxes(d_pair, 1, 2),
        jnp.transpose(dw.reshape(4, DH, C), (2, 0, 1)),
        dwout,
        dwb.T,
    )


def solution(mesh):
    placed = (
        P("rows", None, None),
        P("rows", None, None),
        P("rows", None),
        P(None, None, "heads"),
        P("heads", None),
        P(),
        P("rows", None, None),
    )
    return jax.shard_map(
        shards,
        mesh=mesh,
        in_specs=placed,
        out_specs=(
            P("rows", None, None),
            P("rows", None, "heads"),
            P(None, None, "heads"),
            P("heads", None),
            P(None, "heads"),
        ),
        check_vma=False,
    )
```

```python
import jax
import jax.numpy as jnp
from jax import lax
from jax.experimental import pallas as pl
from jax.experimental.pallas import tpu as pltpu
from jax.sharding import PartitionSpec as P

MESH = pl.DeviceIdType.MESH
F32 = jnp.float32
BF16 = jnp.bfloat16
N = 1024
C = 128
DH = 32
ROWS = 4
OWN = 16
BLK = 256
HALF = 512
EPS = 1e-05
SCALE = 1.0 / DH**0.5


def nn(a, b):
    return lax.dot_general(a, b, (((1,), (0,)), ((), ())), preferred_element_type=F32)


def nt(a, b):
    return lax.dot_general(a, b, (((1,), (1,)), ((), ())), preferred_element_type=F32)


def norm_cols(t):
    cen = t - jnp.mean(t, axis=0, keepdims=True)
    r = lax.rsqrt(jnp.mean(cen * cen, axis=0, keepdims=True) + EPS)
    return cen * r, r


class Sems:
    def __init__(self):
        self.count = 0

    def take(self, n):
        first = self.count
        self.count += n
        return first


SEMS = Sems()
G1 = SEMS.take(1)
GP = SEMS.take(32)
GC = SEMS.take(2)
R1 = SEMS.take(2)
R2 = SEMS.take(16)
R3 = SEMS.take(16)
R4 = SEMS.take(8)
DX1 = SEMS.take(4)
DX2 = SEMS.take(4)
DXA = SEMS.take(16)
W1 = SEMS.take(8)
W2 = SEMS.take(8)
W3 = SEMS.take(8)
B1 = SEMS.take(8)
B2 = SEMS.take(8)
LOW = slice(0, HALF)
HIGH = slice(HALF, N)


def kernel(
    slab_h, pair_h, mask, wt, wout, wbias, dout_h,
    o_dslab, o_dpair, o_dw, o_dwout, o_dwb,
    slab, pair, dout, wn, wbt, wb,
    plane, dbias, xpt, braw, yq, rp, own_bias, ys, rs, xst, zq, z, rhs, natt,
    dkv, gate_s, do_s, s1, r1, s2, r2a, r2b, s3, r3a, r3b, s4, r4, dball,
    dxs, dxr1, dxc, dxr2, dsl, wacc, w1r, wpart, w2r, wtot, fold, bsum, b1r, b2r,
    send, recv, load,
):
    r = lax.axis_index("rows")
    h = lax.axis_index("heads")
    c = lax.rem(r, 2)
    x = lax.rem(r // 2, 4)
    zh = lax.rem(r // 8, 2)
    y = r // 16
    oz = 1 - zh
    odd = lax.rem(h, 2)
    up = h // 2

    def off(a, d):
        return lax.rem(a + d, 4)

    def flip(a, e):
        return 1 - a if e else a

    def peer(dy=0, ez=0, dx=0, ec=0, dh=0):
        row = ((off(y, dy) * 2 + flip(zh, ez)) * 4 + off(x, dx)) * 2 + flip(c, ec)
        return (row, off(h, dh))

    def copy(src, dst, sem, to):
        return pltpu.make_async_remote_copy(
            src_ref=src, dst_ref=dst, send_sem=send.at[sem], recv_sem=recv.at[sem],
            device_id=to, device_id_type=MESH,
        )

    loads = [pltpu.make_async_copy(pair_h.at[4 * k : 4 * k + 4], pair.at[4 * k : 4 * k + 4], load.at[k]) for k in range(4)]
    loads.append(pltpu.make_async_copy(slab_h, slab, load.at[4]))
    loads.append(pltpu.make_async_copy(dout_h, dout, load.at[5]))
    for cp in loads:
        cp.start()

    near = [(dx, ec) for dx in range(4) for ec in range(2) if dx or ec]
    far = [(dy, ez) for dy in range(4) for ez in range(2) if dy or ez]
    peers = [peer(dx=a, ec=b) for a, b in near] + [peer(dy=a, ez=b) for a, b in far]
    for d in (1, 2, 3):
        peers += [peer(dh=d), peer(ez=1, dh=d)]
    barrier = pltpu.get_barrier_semaphore()
    for to in peers:
        pl.semaphore_signal(barrier, inc=1, device_id=to, device_id_type=MESH)

    eye = (
        lax.broadcasted_iota(jnp.int32, (C, C), 0) == lax.broadcasted_iota(jnp.int32, (C, C), 1)
    ).astype(F32).astype(BF16)

    wn[...] = nt(eye, wt[...]).astype(BF16)
    row16 = lax.broadcasted_iota(jnp.int32, (16, C), 0)
    heads = wbias[...].astype(F32)
    wrel = jnp.zeros((16, C), F32)
    for k in range(4):
        wrel = wrel + jnp.where(row16 == off(h + 4, -k), heads[k : k + 1, :], 0.0)
    wb[...] = wrel.astype(BF16)
    wbt[...] = nt(eye, wrel.astype(BF16))
    wbar = jnp.mean(wrel, axis=1, keepdims=True)

    def pair_row(j, _):
        yt, rj = norm_cols(nt(eye, pair[j]))
        xb = yt.astype(BF16)
        xpt[j] = xb
        rp[pl.ds(j, 1), :] = rj
        ys[lax.rem(j, 2)] = yt
        yq[j] = ys[lax.rem(j, 2), pl.ds(pl.multiple_of(h * DH, DH), DH), :]
        raw = nn(wb[...], xb)
        braw[j] = raw
        own_bias[pl.ds(j, 1), :] = raw[0:1, :]
        return 0

    for k in range(4):
        loads[k].wait()
        lax.fori_loop(4 * k, 4 * k + 4, pair_row, 0, unroll=True)
    plane[y, zh, x, c] = own_bias[...].astype(BF16)
    pl.semaphore_wait(barrier, len(peers))

    def gather_first(s):
        zs = flip(zh, s)
        out = []
        for d in (1, 2, 3):
            low = plane.at[y, zs, x, c, :, LOW]
            high = plane.at[y, zs, x, c, :, HIGH]
            out.append(copy(low, low, GP + 16 * s + d, peer(dx=d)))
            out.append(copy(high, high, GP + 16 * s + 4 + d, peer(dy=d)))
        return out

    def gather_second(s):
        zs = flip(zh, s)
        out = []
        for d in (1, 2, 3):
            low = plane.at[y, zs, :, c, :, LOW]
            high = plane.at[:, zs, x, c, :, HIGH]
            out.append(copy(low, low, GP + 16 * s + 8 + d, peer(dy=d)))
            out.append(copy(high, high, GP + 16 * s + 12 + d, peer(dx=d)))
        return out

    def gather_core(s):
        zs = flip(zh, s)
        return copy(plane.at[:, zs, :, c], plane.at[:, zs, :, c], GC + s, peer(ec=1))

    def begin(copies):
        for cp in copies:
            cp.start()

    def end(copies):
        for cp in copies:
            cp.wait()

    g1 = copy(plane.at[y, zh, x, c], plane.at[y, zh, x, c], G1, peer(ez=1))
    g1.start()
    ga1 = gather_first(0)
    begin(ga1)

    def slab_row(i, _):
        yt, ri = norm_cols(nt(eye, slab[i]))
        ys[i] = yt
        rs[pl.ds(i, 1), :] = ri
        xb = yt.astype(BF16)
        xst[i] = xb
        proj = nn(wt[...], xb)
        gate = 1.0 / (1.0 + jnp.exp(-proj[96:128]))
        do = nt(wout[...], dout[i])
        gate_s[i] = gate
        do_s[i] = do
        datt = do * gate
        stack = jnp.concatenate([proj[0:96], datt], axis=0)
        z[i] = stack.T.astype(BF16).reshape(4, 2, 128, C)
        both = jnp.concatenate([proj[0:DH], datt], axis=0).astype(BF16)
        for k in range(8):
            zq[i, k] = both[:, k * 128 : (k + 1) * 128]
        rhs[i, 0:DH, 0:N] = proj[32:64].astype(BF16)
        rhs[i, 96:128, N : 2 * N] = proj[64:96].astype(BF16)
        return 0

    rhs[...] = jnp.zeros(rhs.shape, BF16)
    loads[4].wait()
    loads[5].wait()
    lax.fori_loop(0, 2, slab_row, 0)
    end(ga1)
    ga2 = gather_second(0)
    begin(ga2)
    g1.wait()
    gb1 = gather_first(1)
    begin(gb1)
    lax.fori_loop(2, ROWS, slab_row, 0)
    wacc[...] = jnp.zeros(wacc.shape, F32)
    dkv[...] = jnp.zeros(dkv.shape, F32)
    dbias[...] = jnp.zeros(dbias.shape, F32)
    end(gb1)
    gb2 = gather_second(1)
    begin(gb2)
    end(ga2)
    gac = gather_core(0)
    gac.start()
    gac.wait()

    def block(i, yy, zs):
        keep = mask[pl.ds(i, 1), :] == 1
        two = pl.ds(2 * yy, 2)
        zj = z[i, two, zs].reshape(BLK, C)
        bias = plane[two, zs].reshape(BLK, N).astype(F32)
        logits = nn(zj[:, 0:DH], rhs[i, 0:DH, 0:N]) * SCALE + bias
        logits = jnp.where(keep, logits, -1e9)
        expo = jnp.exp(logits - jnp.max(logits, axis=1, keepdims=True))
        probs = expo * (1.0 / jnp.sum(expo, axis=1, keepdims=True))
        pb = probs.astype(BF16)
        dp = nn(zj[:, 96:128], rhs[i, 96:128, N : 2 * N])
        dl = probs * (dp - jnp.sum(probs * dp, axis=1, keepdims=True))
        dl = jnp.where(keep, dl, 0.0)
        dlb = dl.astype(BF16)
        dbias[two, zs] += dl.reshape(2, 4, 2, OWN, N)
        zall = z[i].reshape(N, C)
        lane = lax.broadcasted_iota(jnp.int32, (BLK, C), 1)
        nat = jnp.where(lane < 64, nn(dlb, zall), nn(pb, zall))
        natt[i, two, zs] = nat.reshape(2, 128, C)
        left = jnp.concatenate([zq[i, 4 * yy + zs], zq[i, 4 * yy + 2 + zs]], axis=1)
        dkv[i, 0:DH, :] += nn(left[0:DH], dlb)
        dkv[i, DH:64, :] += nn(left[DH:64], pb)

    def own_half(t, _):
        block(t // 2, lax.rem(t, 2), zh)
        return 0

    def other_half(t, _):
        block(t // 2, lax.rem(t, 2), oz)
        return 0

    def dx_pair(i):
        to = (r, h + 1 - 2 * odd)
        return copy(dxs.at[i, 1 - odd], dxr1.at[i], DX1 + i, to)

    def dx_cross(i):
        return copy(dxc.at[i], dxr2.at[i], DX2 + i, (r, h + 2 - 4 * up))

    def middle_slab(i):
        dx_pair(i).wait()
        dxc[i] = (dxs[i, odd, 1 - up].astype(F32) + dxr1[i, 1 - up].astype(F32)).astype(BF16)
        dx_cross(i).start()

    def slab_copies(i):
        return [copy(dsl.at[i, h], dsl.at[i, h], DXA + 4 * i + d, peer(dh=d)) for d in (1, 2, 3)]

    def finish_slab(i):
        dx_cross(i).wait()
        g = dxs[i, odd, up].astype(F32) + dxr1[i, up].astype(F32) + dxr2[i].astype(F32)
        cols = pl.ds(pl.multiple_of(h * BLK, BLK), BLK)
        yt = ys[i, :, cols]
        ri = rs[pl.ds(i, 1), cols]
        out = ri * (
            g - jnp.mean(g, axis=0, keepdims=True) - yt * jnp.mean(g * yt, axis=0, keepdims=True)
        )
        dsl[i, h] = out.T.astype(BF16)
        begin(slab_copies(i))

    def finish_row(i):
        nat = natt[i].reshape(N, C).T
        gate = gate_s[i]
        do = do_s[i]
        att = nat[64:96]
        gated = (gate * att).astype(BF16)
        dgate = do * att * gate * (1.0 - gate)
        grads = jnp.concatenate(
            [nat[32:64] * SCALE, dkv[i, 0:DH, :] * SCALE, dkv[i, DH:64, :], dgate], axis=0
        ).astype(BF16)
        dx = nn(wn[...], grads).astype(BF16)
        for q in range(4):
            dxs[i, q % 2, q // 2] = dx[:, q * BLK : (q + 1) * BLK]
        dx_pair(i).start()
        wacc[0:C, :] += nt(grads, xst[i])
        wacc[C : C + DH, :] += nn(gated, dout[i])

    def sum_core(s):
        zs = flip(zh, s)
        s1[s] = dbias[:, zs, :, 1 - c].astype(BF16)
        return copy(s1.at[s], r1.at[s], R1 + s, peer(ec=1))

    def sum_first(s):
        zs = flip(zh, s)
        for yy in range(4):
            total = dbias[yy, zs, :, c] + r1[s, yy].astype(F32)
            dbias[yy, zs, :, c] = total
            s2[s, yy] = total.astype(BF16)
        out = []
        for d in (1, 2, 3):
            low = s2.at[s, off(y, d), :, :, LOW]
            high = s2.at[s, :, off(x, d), :, HIGH]
            out.append(copy(low, r2a.at[s, d], R2 + 8 * s + d, peer(dy=d)))
            out.append(copy(high, r2b.at[s, d], R2 + 8 * s + 4 + d, peer(dx=d)))
        return out

    def sum_second(s):
        zs = flip(zh, s)
        low = dbias[y, zs, :, c, :, LOW]
        high = dbias[:, zs, x, c, :, HIGH]
        for d in (1, 2, 3):
            low = low + r2a[s, d].astype(F32)
            high = high + r2b[s, d].astype(F32)
        s3[s, 0] = low.astype(BF16)
        s3[s, 1] = high.astype(BF16)
        dbias[y, zs, :, c, :, LOW] = low
        dbias[:, zs, x, c, :, HIGH] = high
        out = []
        for d in (1, 2, 3):
            out.append(copy(s3.at[s, 0, off(x, d)], r3a.at[s, d], R3 + 8 * s + d, peer(dx=d)))
            out.append(copy(s3.at[s, 1, off(y, d)], r3b.at[s, d], R3 + 8 * s + 4 + d, peer(dy=d)))
        return out

    def sum_last(s):
        zs = flip(zh, s)
        low = dbias[y, zs, x, c, :, LOW]
        high = dbias[y, zs, x, c, :, HIGH]
        for d in (1, 2, 3):
            low = low + r3a[s, d].astype(F32)
            high = high + r3b[s, d].astype(F32)
        both = jnp.concatenate([low, high], axis=1)
        s4[s] = both.astype(BF16)
        out = []
        for d in range(4):
            if s or d:
                out.append(copy(s4.at[s], r4.at[s, d], R4 + 4 * s + d, peer(ez=s, dh=d)))
        return both, out

    lax.fori_loop(0, 4, own_half, 0, unroll=2)
    end(gb2)
    gbc = gather_core(1)
    gbc.start()
    gbc.wait()
    lax.fori_loop(0, 2, other_half, 0, unroll=2)
    finish_row(0)
    lax.fori_loop(4, 8, own_half, 0, unroll=2)
    ra1 = sum_core(0)
    ra1.start()
    middle_slab(0)
    lax.fori_loop(2, 4, other_half, 0, unroll=2)
    finish_row(1)
    ra1.wait()
    ra2 = sum_first(0)
    begin(ra2)
    finish_slab(0)
    lax.fori_loop(4, 6, other_half, 0, unroll=2)
    finish_row(2)
    end(ra2)
    ra3 = sum_second(0)
    begin(ra3)
    middle_slab(1)
    lax.fori_loop(6, 8, other_half, 0, unroll=2)
    rb1 = sum_core(1)
    rb1.start()
    finish_row(3)
    chunk = 24

    def wslice(k):
        return pl.ds(pl.multiple_of(k * chunk, 8), chunk)

    def wid(dx, ec):
        return off(x, dx) * 2 + flip(c, ec)

    w1 = [
        copy(wacc.at[wslice(wid(a, b))], w1r.at[2 * a + b], W1 + 2 * a + b, peer(dx=a, ec=b))
        for a, b in near
    ]
    end(ra3)
    own, ra4 = sum_last(0)
    own_bias[...] = own
    begin(ra4)
    rb1.wait()
    rb2 = sum_first(1)
    begin(rb2)
    begin(w1)
    middle_slab(2)
    finish_slab(1)
    end(w1)
    part = wacc[wslice(wid(0, 0)), :]
    for a, b in near:
        part = part + w1r[2 * a + b]
    wpart[...] = part
    w2 = [copy(wpart, w2r.at[2 * a + b], W2 + 2 * a + b, peer(dy=a, ez=b)) for a, b in far]
    begin(w2)
    middle_slab(3)
    end(rb2)
    rb3 = sum_second(1)
    begin(rb3)
    finish_slab(2)
    end(rb3)
    _, rb4 = sum_last(1)
    begin(rb4)
    finish_slab(3)
    end(w2)
    part = wpart[...]
    for a, b in far:
        part = part + w2r[2 * a + b]
    wtot[wslice(wid(0, 0)), :] = part
    w3 = [
        copy(
            wtot.at[wslice(wid(0, 0))], wtot.at[wslice(wid(0, 0))], W3 + 2 * a + b,
            peer(dx=a, ec=b),
        )
        for a, b in near
    ]
    begin(w3)
    end(ra4)
    end(rb4)

    db = own_bias[...] + r4[1, 0].astype(F32)
    own_bias[...] = db
    dball[:, 0, :] = db
    for d in (1, 2, 3):
        dball[:, d, :] = r4[0, d].astype(F32) + r4[1, d].astype(F32)
    dball[:, 4:16, :] = jnp.zeros((OWN, 12, N), F32)

    def wb_part(k, _):
        sub = pl.ds(pl.multiple_of(k * 32, 32), 32)
        acc = xpt[0, sub, :].astype(F32) * own_bias[0:1, :]
        for j in range(1, OWN):
            acc = acc + xpt[j, sub, :].astype(F32) * own_bias[j : j + 1, :]
        total = acc[:, 0:128]
        for q in range(1, 8):
            total = total + acc[:, q * 128 : (q + 1) * 128]
        fold[sub, :] = total
        return 0

    lax.fori_loop(0, 4, wb_part, 0)
    total = fold[...]
    hi = total.astype(BF16)
    mid = (total - hi.astype(F32)).astype(BF16)
    lo = (total - hi.astype(F32) - mid.astype(F32)).astype(BF16)
    ones = jnp.ones((16, C), F32).astype(BF16)
    bsum[0] = (nt(ones, hi) + nt(ones, mid) + nt(ones, lo))[0:8]
    b1 = [copy(bsum.at[0], b1r.at[2 * a + b], B1 + 2 * a + b, peer(dx=a, ec=b)) for a, b in near]
    begin(b1)

    def dpair_row(j, _):
        dbj = dball[j]
        wq = wbt[pl.ds(pl.multiple_of(h * DH, DH), DH), :].astype(BF16)
        g = nn(wq, dbj.astype(BF16))
        first = jnp.sum(dbj * wbar, axis=0, keepdims=True)
        second = jnp.sum(dbj * braw[j], axis=0, keepdims=True) * (1.0 / C)
        o_dpair[j] = (rp[pl.ds(j, 1), :] * (g - first - yq[j] * second)).astype(BF16)
        return 0

    lax.fori_loop(0, 8, dpair_row, 0, unroll=4)
    end(b1)
    part = bsum[0]
    for a, b in near:
        part = part + b1r[2 * a + b]
    bsum[1] = part
    b2 = [copy(bsum.at[1], b2r.at[2 * a + b], B2 + 2 * a + b, peer(dy=a, ez=b)) for a, b in far]
    begin(b2)
    lax.fori_loop(8, OWN, dpair_row, 0, unroll=4)
    end(w3)
    o_dw[...] = wtot[0:C, :]
    o_dwout[...] = wtot[C : C + DH, :]
    for i in range(ROWS):
        end(slab_copies(i))
        for q in range(4):
            o_dslab[i, q * BLK : (q + 1) * BLK, :] = dsl[i, q]
    end(b2)
    part = bsum[1]
    for a, b in far:
        part = part + b2r[2 * a + b]
    o_dwb[...] = part[0:1, :]


def scratch():
    v = pltpu.VMEM
    return [
        v((ROWS, N, C), BF16),
        v((OWN, N, C), BF16),
        v((ROWS, N, C), BF16),
        v((C, C), BF16),
        v((C, 16), F32),
        v((16, C), BF16),
        v((4, 2, 4, 2, OWN, N), BF16),
        v((4, 2, 4, 2, OWN, N), F32),
        v((OWN, C, N), BF16),
        v((OWN, OWN, N), F32),
        v((OWN, DH, N), F32),
        v((OWN, N), F32),
        v((OWN, N), F32),
        v((ROWS, C, N), F32),
        v((8, N), F32),
        v((ROWS, C, N), BF16),
        v((ROWS, 8, 64, 128), BF16),
        v((ROWS, 4, 2, 128, C), BF16),
        v((ROWS, C, 2 * N), BF16),
        v((ROWS, 4, 2, 128, C), F32),
        v((ROWS, 64, N), F32),
        v((ROWS, DH, N), F32),
        v((ROWS, DH, N), F32),
        v((2, 4, 4, OWN, N), BF16),
        v((2, 4, 4, OWN, N), BF16),
        v((2, 4, 4, OWN, N), BF16),
        v((2, 4, 4, OWN, HALF), BF16),
        v((2, 4, 4, OWN, HALF), BF16),
        v((2, 2, 4, OWN, HALF), BF16),
        v((2, 4, OWN, HALF), BF16),
        v((2, 4, OWN, HALF), BF16),
        v((2, OWN, N), BF16),
        v((2, 4, OWN, N), BF16),
        v((OWN, OWN, N), F32),
        v((ROWS, 2, 2, C, BLK), BF16),
        v((ROWS, 2, C, BLK), BF16),
        v((ROWS, C, BLK), BF16),
        v((ROWS, C, BLK), BF16),
        v((ROWS, 4, BLK, C), BF16),
        v((192, C), F32),
        v((8, 24, C), F32),
        v((24, C), F32),
        v((8, 24, C), F32),
        v((192, C), F32),
        v((C, C), F32),
        v((2, 8, C), F32),
        v((8, 8, C), F32),
        v((8, 8, C), F32),
        pltpu.SemaphoreType.DMA((SEMS.count,)),
        pltpu.SemaphoreType.DMA((SEMS.count,)),
        pltpu.SemaphoreType.DMA((6,)),
    ]


def hand_on(*refs):
    n = len(refs) // 2
    for k in range(n):
        refs[n + k][...] = refs[k][...]


def shards(slab, pair, pair_mask, w_qkvg, w_out, w_bias, d_out):
    wt = jnp.transpose(w_qkvg, (1, 2, 0)).reshape(C, C)
    vm = pl.BlockSpec(memory_space=pltpu.VMEM)
    anywhere = pl.BlockSpec(memory_space=pl.ANY)
    shapes = (
        jax.ShapeDtypeStruct((ROWS, N, C), BF16),
        jax.ShapeDtypeStruct((OWN, DH, N), BF16),
        jax.ShapeDtypeStruct((C, C), F32),
        jax.ShapeDtypeStruct((DH, C), F32),
        jax.ShapeDtypeStruct((1, C), F32),
    )
    outs = pl.pallas_call(
        kernel,
        out_shape=shapes,
        in_specs=[anywhere, anywhere, vm, vm, vm, vm, anywhere],
        out_specs=(vm,) * 5,
        scratch_shapes=scratch(),
        compiler_params=pltpu.CompilerParams(
            collective_id=0, has_side_effects=True, vmem_limit_bytes=60 * 1024 * 1024
        ),
    )(slab, pair, pair_mask, wt, w_out, w_bias.T, d_out)
    blocks = [
        pl.BlockSpec((1, N, C), lambda k: (k, 0, 0)),
        pl.BlockSpec((4, DH, N), lambda k: (k, 0, 0)),
        pl.BlockSpec((DH, C), lambda k: (k, 0)),
        pl.BlockSpec((8, C), lambda k: (k, 0)),
        pl.BlockSpec((1, C), lambda k: (0, 0)),
    ]
    d_slab, d_pair, dw, dwout, dwb = pl.pallas_call(
        hand_on,
        grid=(4,),
        out_shape=shapes,
        in_specs=blocks,
        out_specs=blocks,
    )(*outs)
    return (
        d_slab,
        jnp.swapaxes(d_pair, 1, 2),
        jnp.transpose(dw.reshape(4, DH, C), (2, 0, 1)),
        dwout,
        dwb.T,
    )


def solution(mesh):
    placed = (
        P("rows", None, None),
        P("rows", None, None),
        P("rows", None),
        P(None, None, "heads"),
        P("heads", None),
        P(),
        P("rows", None, None),
    )
    return jax.shard_map(
        shards,
        mesh=mesh,
        in_specs=placed,
        out_specs=(
            P("rows", None, None),
            P("rows", None, "heads"),
            P(None, None, "heads"),
            P("heads", None),
            P(None, "heads"),
        ),
        check_vma=False,
    )
```

```python
import jax
import jax.numpy as jnp
from jax import lax
from jax.experimental import pallas as pl
from jax.experimental.pallas import tpu as pltpu
from jax.sharding import PartitionSpec as P

MESH = pl.DeviceIdType.MESH
F32 = jnp.float32
BF16 = jnp.bfloat16
N = 1024
C = 128
DH = 32
ROWS = 4
OWN = 16
BLK = 256
HALF = 512
EPS = 1e-05
SCALE = 1.0 / DH**0.5


def nn(a, b):
    return lax.dot_general(a, b, (((1,), (0,)), ((), ())), preferred_element_type=F32)


def nt(a, b):
    return lax.dot_general(a, b, (((1,), (1,)), ((), ())), preferred_element_type=F32)


def norm_cols(t):
    cen = t - jnp.mean(t, axis=0, keepdims=True)
    r = lax.rsqrt(jnp.mean(cen * cen, axis=0, keepdims=True) + EPS)
    return cen * r, r


class Sems:
    def __init__(self):
        self.count = 0

    def take(self, n):
        first = self.count
        self.count += n
        return first


SEMS = Sems()
G1 = SEMS.take(1)
GP = SEMS.take(32)
GC = SEMS.take(2)
R1 = SEMS.take(2)
R2 = SEMS.take(16)
R3 = SEMS.take(16)
R4 = SEMS.take(8)
DX1 = SEMS.take(4)
DX2 = SEMS.take(4)
DXA = SEMS.take(16)
W1 = SEMS.take(8)
W2 = SEMS.take(8)
W3 = SEMS.take(8)
B1 = SEMS.take(8)
B2 = SEMS.take(8)
LOW = slice(0, HALF)
HIGH = slice(HALF, N)


def kernel(
    slab_h, pair_h, mask, wt, wout, wbias, dout_h,
    o_dslab, o_dpair, o_dw, o_dwout, o_dwb,
    slab, pair, dout, wn, wbt, wb,
    plane, dbias, xpt, braw, yq, rp, own_bias, ys, rs, xst, zq, z, rhs, natt,
    dkv, gate_s, do_s, s1, r1, s2, r2a, r2b, s3, r3a, r3b, s4, r4, dball,
    dxs, dxr1, dxc, dxr2, dsl, dpair, wacc, w1r, wpart, w2r, wtot, fold, bsum, b1r, b2r,
    send, recv, load,
):
    r = lax.axis_index("rows")
    h = lax.axis_index("heads")
    c = lax.rem(r, 2)
    x = lax.rem(r // 2, 4)
    zh = lax.rem(r // 8, 2)
    y = r // 16
    oz = 1 - zh
    odd = lax.rem(h, 2)
    up = h // 2

    def off(a, d):
        return lax.rem(a + d, 4)

    def flip(a, e):
        return 1 - a if e else a

    def peer(dy=0, ez=0, dx=0, ec=0, dh=0):
        row = ((off(y, dy) * 2 + flip(zh, ez)) * 4 + off(x, dx)) * 2 + flip(c, ec)
        return (row, off(h, dh))

    def copy(src, dst, sem, to):
        return pltpu.make_async_remote_copy(
            src_ref=src, dst_ref=dst, send_sem=send.at[sem], recv_sem=recv.at[sem],
            device_id=to, device_id_type=MESH,
        )

    loads = [pltpu.make_async_copy(pair_h.at[4 * k : 4 * k + 4], pair.at[4 * k : 4 * k + 4], load.at[k]) for k in range(4)]
    loads.append(pltpu.make_async_copy(slab_h, slab, load.at[4]))
    loads.append(pltpu.make_async_copy(dout_h, dout, load.at[5]))
    for cp in loads:
        cp.start()

    near = [(dx, ec) for dx in range(4) for ec in range(2) if dx or ec]
    far = [(dy, ez) for dy in range(4) for ez in range(2) if dy or ez]
    peers = [peer(dx=a, ec=b) for a, b in near] + [peer(dy=a, ez=b) for a, b in far]
    for d in (1, 2, 3):
        peers += [peer(dh=d), peer(ez=1, dh=d)]
    barrier = pltpu.get_barrier_semaphore()
    for to in peers:
        pl.semaphore_signal(barrier, inc=1, device_id=to, device_id_type=MESH)

    eye = (
        lax.broadcasted_iota(jnp.int32, (C, C), 0) == lax.broadcasted_iota(jnp.int32, (C, C), 1)
    ).astype(F32).astype(BF16)

    wn[...] = nt(eye, wt[...]).astype(BF16)
    row16 = lax.broadcasted_iota(jnp.int32, (16, C), 0)
    heads = wbias[...].astype(F32)
    wrel = jnp.zeros((16, C), F32)
    for k in range(4):
        wrel = wrel + jnp.where(row16 == off(h + 4, -k), heads[k : k + 1, :], 0.0)
    wb[...] = wrel.astype(BF16)
    wbt[...] = nt(eye, wrel.astype(BF16))
    wbar = jnp.mean(wrel, axis=1, keepdims=True)

    def pair_row(j, _):
        yt, rj = norm_cols(nt(eye, pair[j]))
        xb = yt.astype(BF16)
        xpt[j] = xb
        rp[pl.ds(j, 1), :] = rj
        ys[lax.rem(j, 2)] = yt
        yq[j] = ys[lax.rem(j, 2), pl.ds(pl.multiple_of(h * DH, DH), DH), :]
        raw = nn(wb[...], xb)
        braw[j] = raw
        own_bias[pl.ds(j, 1), :] = raw[0:1, :]
        return 0

    for k in range(4):
        loads[k].wait()
        lax.fori_loop(4 * k, 4 * k + 4, pair_row, 0, unroll=True)
    plane[y, zh, x, c] = own_bias[...].astype(BF16)
    pl.semaphore_wait(barrier, len(peers))

    def gather_first(s):
        zs = flip(zh, s)
        out = []
        for d in (1, 2, 3):
            low = plane.at[y, zs, x, c, :, LOW]
            high = plane.at[y, zs, x, c, :, HIGH]
            out.append(copy(low, low, GP + 16 * s + d, peer(dx=d)))
            out.append(copy(high, high, GP + 16 * s + 4 + d, peer(dy=d)))
        return out

    def gather_second(s):
        zs = flip(zh, s)
        out = []
        for d in (1, 2, 3):
            low = plane.at[y, zs, :, c, :, LOW]
            high = plane.at[:, zs, x, c, :, HIGH]
            out.append(copy(low, low, GP + 16 * s + 8 + d, peer(dy=d)))
            out.append(copy(high, high, GP + 16 * s + 12 + d, peer(dx=d)))
        return out

    def gather_core(s):
        zs = flip(zh, s)
        return copy(plane.at[:, zs, :, c], plane.at[:, zs, :, c], GC + s, peer(ec=1))

    def begin(copies):
        for cp in copies:
            cp.start()

    def end(copies):
        for cp in copies:
            cp.wait()

    g1 = copy(plane.at[y, zh, x, c], plane.at[y, zh, x, c], G1, peer(ez=1))
    g1.start()
    ga1 = gather_first(0)
    begin(ga1)

    def slab_row(i, _):
        yt, ri = norm_cols(nt(eye, slab[i]))
        ys[i] = yt
        rs[pl.ds(i, 1), :] = ri
        xb = yt.astype(BF16)
        xst[i] = xb
        proj = nn(wt[...], xb)
        gate = 1.0 / (1.0 + jnp.exp(-proj[96:128]))
        do = nt(wout[...], dout[i])
        gate_s[i] = gate
        do_s[i] = do
        datt = do * gate
        stack = jnp.concatenate([proj[0:96], datt], axis=0)
        z[i] = stack.T.astype(BF16).reshape(4, 2, 128, C)
        both = jnp.concatenate([proj[0:DH], datt], axis=0).astype(BF16)
        for k in range(8):
            zq[i, k] = both[:, k * 128 : (k + 1) * 128]
        rhs[i, 0:DH, 0:N] = proj[32:64].astype(BF16)
        rhs[i, 96:128, N : 2 * N] = proj[64:96].astype(BF16)
        return 0

    rhs[...] = jnp.zeros(rhs.shape, BF16)
    loads[4].wait()
    loads[5].wait()
    lax.fori_loop(0, 2, slab_row, 0)
    end(ga1)
    ga2 = gather_second(0)
    begin(ga2)
    g1.wait()
    gb1 = gather_first(1)
    begin(gb1)
    lax.fori_loop(2, ROWS, slab_row, 0)
    wacc[...] = jnp.zeros(wacc.shape, F32)
    dkv[...] = jnp.zeros(dkv.shape, F32)
    dbias[...] = jnp.zeros(dbias.shape, F32)
    end(gb1)
    gb2 = gather_second(1)
    begin(gb2)
    end(ga2)
    gac = gather_core(0)
    gac.start()
    gac.wait()

    def block(i, yy, zs):
        keep = mask[pl.ds(i, 1), :] == 1
        two = pl.ds(2 * yy, 2)
        zj = z[i, two, zs].reshape(BLK, C)
        bias = plane[two, zs].reshape(BLK, N).astype(F32)
        logits = nn(zj[:, 0:DH], rhs[i, 0:DH, 0:N]) * SCALE + bias
        logits = jnp.where(keep, logits, -1e9)
        expo = jnp.exp(logits - jnp.max(logits, axis=1, keepdims=True))
        probs = expo * (1.0 / jnp.sum(expo, axis=1, keepdims=True))
        pb = probs.astype(BF16)
        dp = nn(zj[:, 96:128], rhs[i, 96:128, N : 2 * N])
        dl = probs * (dp - jnp.sum(probs * dp, axis=1, keepdims=True))
        dl = jnp.where(keep, dl, 0.0)
        dlb = dl.astype(BF16)
        dbias[two, zs] += dl.reshape(2, 4, 2, OWN, N)
        zall = z[i].reshape(N, C)
        lane = lax.broadcasted_iota(jnp.int32, (BLK, C), 1)
        nat = jnp.where(lane < 64, nn(dlb, zall), nn(pb, zall))
        natt[i, two, zs] = nat.reshape(2, 128, C)
        left = jnp.concatenate([zq[i, 4 * yy + zs], zq[i, 4 * yy + 2 + zs]], axis=1)
        dkv[i, 0:DH, :] += nn(left[0:DH], dlb)
        dkv[i, DH:64, :] += nn(left[DH:64], pb)

    def own_half(t, _):
        block(t // 2, lax.rem(t, 2), zh)
        return 0

    def other_half(t, _):
        block(t // 2, lax.rem(t, 2), oz)
        return 0

    def dx_pair(i):
        to = (r, h + 1 - 2 * odd)
        return copy(dxs.at[i, 1 - odd], dxr1.at[i], DX1 + i, to)

    def dx_cross(i):
        return copy(dxc.at[i], dxr2.at[i], DX2 + i, (r, h + 2 - 4 * up))

    def middle_slab(i):
        dx_pair(i).wait()
        dxc[i] = (dxs[i, odd, 1 - up].astype(F32) + dxr1[i, 1 - up].astype(F32)).astype(BF16)
        dx_cross(i).start()

    def slab_copies(i):
        return [copy(dsl.at[i, h], dsl.at[i, h], DXA + 4 * i + d, peer(dh=d)) for d in (1, 2, 3)]

    def finish_slab(i):
        dx_cross(i).wait()
        g = dxs[i, odd, up].astype(F32) + dxr1[i, up].astype(F32) + dxr2[i].astype(F32)
        cols = pl.ds(pl.multiple_of(h * BLK, BLK), BLK)
        yt = ys[i, :, cols]
        ri = rs[pl.ds(i, 1), cols]
        out = ri * (
            g - jnp.mean(g, axis=0, keepdims=True) - yt * jnp.mean(g * yt, axis=0, keepdims=True)
        )
        dsl[i, h] = out.T.astype(BF16)
        begin(slab_copies(i))

    def finish_row(i):
        nat = natt[i].reshape(N, C).T
        gate = gate_s[i]
        do = do_s[i]
        att = nat[64:96]
        gated = (gate * att).astype(BF16)
        dgate = do * att * gate * (1.0 - gate)
        grads = jnp.concatenate(
            [nat[32:64] * SCALE, dkv[i, 0:DH, :] * SCALE, dkv[i, DH:64, :], dgate], axis=0
        ).astype(BF16)
        dx = nn(wn[...], grads).astype(BF16)
        for q in range(4):
            dxs[i, q % 2, q // 2] = dx[:, q * BLK : (q + 1) * BLK]
        dx_pair(i).start()
        wacc[0:C, :] += nt(grads, xst[i])
        wacc[C : C + DH, :] += nn(gated, dout[i])

    def sum_core(s):
        zs = flip(zh, s)
        s1[s] = dbias[:, zs, :, 1 - c].astype(BF16)
        return copy(s1.at[s], r1.at[s], R1 + s, peer(ec=1))

    def sum_first(s):
        zs = flip(zh, s)
        for yy in range(4):
            total = dbias[yy, zs, :, c] + r1[s, yy].astype(F32)
            dbias[yy, zs, :, c] = total
            s2[s, yy] = total.astype(BF16)
        out = []
        for d in (1, 2, 3):
            low = s2.at[s, off(y, d), :, :, LOW]
            high = s2.at[s, :, off(x, d), :, HIGH]
            out.append(copy(low, r2a.at[s, d], R2 + 8 * s + d, peer(dy=d)))
            out.append(copy(high, r2b.at[s, d], R2 + 8 * s + 4 + d, peer(dx=d)))
        return out

    def sum_second(s):
        zs = flip(zh, s)
        low = dbias[y, zs, :, c, :, LOW]
        high = dbias[:, zs, x, c, :, HIGH]
        for d in (1, 2, 3):
            low = low + r2a[s, d].astype(F32)
            high = high + r2b[s, d].astype(F32)
        s3[s, 0] = low.astype(BF16)
        s3[s, 1] = high.astype(BF16)
        dbias[y, zs, :, c, :, LOW] = low
        dbias[:, zs, x, c, :, HIGH] = high
        out = []
        for d in (1, 2, 3):
            out.append(copy(s3.at[s, 0, off(x, d)], r3a.at[s, d], R3 + 8 * s + d, peer(dx=d)))
            out.append(copy(s3.at[s, 1, off(y, d)], r3b.at[s, d], R3 + 8 * s + 4 + d, peer(dy=d)))
        return out

    def sum_last(s):
        zs = flip(zh, s)
        low = dbias[y, zs, x, c, :, LOW]
        high = dbias[y, zs, x, c, :, HIGH]
        for d in (1, 2, 3):
            low = low + r3a[s, d].astype(F32)
            high = high + r3b[s, d].astype(F32)
        both = jnp.concatenate([low, high], axis=1)
        s4[s] = both.astype(BF16)
        out = []
        for d in range(4):
            if s or d:
                out.append(copy(s4.at[s], r4.at[s, d], R4 + 4 * s + d, peer(ez=s, dh=d)))
        return both, out

    def own_row(i):
        lax.fori_loop(2 * i, 2 * i + 2, own_half, 0, unroll=2)

    def other_row(i):
        lax.fori_loop(2 * i, 2 * i + 2, other_half, 0, unroll=2)

    lax.fori_loop(0, 4, own_half, 0, unroll=2)
    end(gb2)
    gbc = gather_core(1)
    gbc.start()
    own_row(2)
    gbc.wait()
    for i in range(3):
        other_row(i)
        finish_row(i)
    middle_slab(0)
    own_row(3)
    middle_slab(1)
    ra1 = sum_core(0)
    ra1.start()
    other_row(3)
    rb1 = sum_core(1)
    rb1.start()
    finish_row(3)
    chunk = 24

    def wslice(k):
        return pl.ds(pl.multiple_of(k * chunk, 8), chunk)

    def wid(dx, ec):
        return off(x, dx) * 2 + flip(c, ec)

    w1 = [
        copy(wacc.at[wslice(wid(a, b))], w1r.at[2 * a + b], W1 + 2 * a + b, peer(dx=a, ec=b))
        for a, b in near
    ]
    rb1.wait()
    rb2 = sum_first(1)
    begin(rb2)
    begin(w1)
    middle_slab(2)
    finish_slab(0)
    finish_slab(1)
    ra1.wait()
    ra2 = sum_first(0)
    middle_slab(3)
    end(rb2)
    rb3 = sum_second(1)
    begin(rb3)
    begin(ra2)
    finish_slab(2)
    end(w1)
    part = wacc[wslice(wid(0, 0)), :]
    for a, b in near:
        part = part + w1r[2 * a + b]
    wpart[...] = part
    w2 = [copy(wpart, w2r.at[2 * a + b], W2 + 2 * a + b, peer(dy=a, ez=b)) for a, b in far]
    begin(w2)
    end(rb3)
    _, rb4 = sum_last(1)
    begin(rb4)
    finish_slab(3)
    end(ra2)
    ra3 = sum_second(0)
    begin(ra3)
    end(w2)
    part = wpart[...]
    for a, b in far:
        part = part + w2r[2 * a + b]
    wtot[wslice(wid(0, 0)), :] = part
    w3 = [
        copy(
            wtot.at[wslice(wid(0, 0))], wtot.at[wslice(wid(0, 0))], W3 + 2 * a + b,
            peer(dx=a, ec=b),
        )
        for a, b in near
    ]
    begin(w3)
    end(ra3)
    own, ra4 = sum_last(0)
    begin(ra4)
    rb4[0].wait()

    db = own + r4[1, 0].astype(F32)
    own_bias[...] = db
    dball[:, 0, :] = db

    def wb_part(k, _):
        sub = pl.ds(pl.multiple_of(k * 32, 32), 32)
        acc = xpt[0, sub, :].astype(F32) * own_bias[0:1, :]
        for j in range(1, OWN):
            acc = acc + xpt[j, sub, :].astype(F32) * own_bias[j : j + 1, :]
        total = acc[:, 0:128]
        for q in range(1, 8):
            total = total + acc[:, q * 128 : (q + 1) * 128]
        fold[sub, :] = total
        return 0

    lax.fori_loop(0, 4, wb_part, 0)
    total = fold[...]
    hi = total.astype(BF16)
    mid = (total - hi.astype(F32)).astype(BF16)
    lo = (total - hi.astype(F32) - mid.astype(F32)).astype(BF16)
    ones = jnp.ones((16, C), F32).astype(BF16)
    bsum[0] = (nt(ones, hi) + nt(ones, mid) + nt(ones, lo))[0:8]
    b1 = [copy(bsum.at[0], b1r.at[2 * a + b], B1 + 2 * a + b, peer(dx=a, ec=b)) for a, b in near]
    begin(b1)

    def dpair_row(j, _):
        dbj = dball[j]
        wq = wbt[pl.ds(pl.multiple_of(h * DH, DH), DH), :].astype(BF16)
        g = nn(wq, dbj.astype(BF16))
        first = jnp.sum(dbj * wbar, axis=0, keepdims=True)
        second = jnp.sum(dbj * braw[j], axis=0, keepdims=True) * (1.0 / C)
        dpair[j] = (rp[pl.ds(j, 1), :] * (g - first - yq[j] * second)).astype(BF16)
        return 0

    end(ra4)
    end(rb4[1:])
    for d in (1, 2, 3):
        dball[:, d, :] = r4[0, d].astype(F32) + r4[1, d].astype(F32)
    dball[:, 4:16, :] = jnp.zeros((OWN, 12, N), F32)
    lax.fori_loop(0, 8, dpair_row, 0, unroll=4)
    out_low = pltpu.make_async_copy(dpair.at[0:8], o_dpair.at[0:8], load.at[4])
    out_low.start()
    end(b1)
    part = bsum[0]
    for a, b in near:
        part = part + b1r[2 * a + b]
    bsum[1] = part
    b2 = [copy(bsum.at[1], b2r.at[2 * a + b], B2 + 2 * a + b, peer(dy=a, ez=b)) for a, b in far]
    begin(b2)
    lax.fori_loop(8, OWN, dpair_row, 0, unroll=4)
    out_high = pltpu.make_async_copy(dpair.at[8:16], o_dpair.at[8:16], load.at[5])
    out_high.start()
    end(w3)
    o_dw[...] = wtot[0:C, :]
    o_dwout[...] = wtot[C : C + DH, :]
    slab_out = [pltpu.make_async_copy(dsl.at[i], o_dslab.at[i], load.at[i]) for i in range(ROWS)]
    for i in range(ROWS):
        end(slab_copies(i))
        slab_out[i].start()
    end(b2)
    part = bsum[1]
    for a, b in far:
        part = part + b2r[2 * a + b]
    o_dwb[...] = part[0:1, :]
    for cp in slab_out + [out_low, out_high]:
        cp.wait()


def scratch():
    v = pltpu.VMEM
    return [
        v((ROWS, N, C), BF16),
        v((OWN, N, C), BF16),
        v((ROWS, N, C), BF16),
        v((C, C), BF16),
        v((C, 16), F32),
        v((16, C), BF16),
        v((4, 2, 4, 2, OWN, N), BF16),
        v((4, 2, 4, 2, OWN, N), F32),
        v((OWN, C, N), BF16),
        v((OWN, OWN, N), F32),
        v((OWN, DH, N), F32),
        v((OWN, N), F32),
        v((OWN, N), F32),
        v((ROWS, C, N), F32),
        v((8, N), F32),
        v((ROWS, C, N), BF16),
        v((ROWS, 8, 64, 128), BF16),
        v((ROWS, 4, 2, 128, C), BF16),
        v((ROWS, C, 2 * N), BF16),
        v((ROWS, 4, 2, 128, C), F32),
        v((ROWS, 64, N), F32),
        v((ROWS, DH, N), F32),
        v((ROWS, DH, N), F32),
        v((2, 4, 4, OWN, N), BF16),
        v((2, 4, 4, OWN, N), BF16),
        v((2, 4, 4, OWN, N), BF16),
        v((2, 4, 4, OWN, HALF), BF16),
        v((2, 4, 4, OWN, HALF), BF16),
        v((2, 2, 4, OWN, HALF), BF16),
        v((2, 4, OWN, HALF), BF16),
        v((2, 4, OWN, HALF), BF16),
        v((2, OWN, N), BF16),
        v((2, 4, OWN, N), BF16),
        v((OWN, OWN, N), F32),
        v((ROWS, 2, 2, C, BLK), BF16),
        v((ROWS, 2, C, BLK), BF16),
        v((ROWS, C, BLK), BF16),
        v((ROWS, C, BLK), BF16),
        v((ROWS, 4, BLK, C), BF16),
        v((OWN, DH, N), BF16),
        v((192, C), F32),
        v((8, 24, C), F32),
        v((24, C), F32),
        v((8, 24, C), F32),
        v((192, C), F32),
        v((C, C), F32),
        v((2, 8, C), F32),
        v((8, 8, C), F32),
        v((8, 8, C), F32),
        pltpu.SemaphoreType.DMA((SEMS.count,)),
        pltpu.SemaphoreType.DMA((SEMS.count,)),
        pltpu.SemaphoreType.DMA((6,)),
    ]


def hand_on(*refs):
    outs, held, sem = refs[5:10], refs[10:15], refs[15]
    first, second = [], []
    for k in range(5):
        pieces = 4 if k < 2 else 1
        for q in range(pieces):
            size = held[k].shape[0] // pieces
            part = pl.ds(q * size, size)
            one = sem.at[0, 4 * k + q]
            two = sem.at[1, 4 * k + q]
            first.append(pltpu.make_async_copy(refs[k].at[part], held[k].at[part], one))
            second.append(pltpu.make_async_copy(held[k].at[part], outs[k].at[part], two))
    for cp in first:
        cp.start()
    for cp, then in zip(first, second):
        cp.wait()
        then.start()
    for cp in second:
        cp.wait()


def shards(slab, pair, pair_mask, w_qkvg, w_out, w_bias, d_out):
    wt = jnp.transpose(w_qkvg, (1, 2, 0)).reshape(C, C)
    vm = pl.BlockSpec(memory_space=pltpu.VMEM)
    anywhere = pl.BlockSpec(memory_space=pl.ANY)
    shapes = (
        jax.ShapeDtypeStruct((ROWS, 4, BLK, C), BF16),
        jax.ShapeDtypeStruct((OWN, DH, N), BF16),
        jax.ShapeDtypeStruct((C, C), F32),
        jax.ShapeDtypeStruct((DH, C), F32),
        jax.ShapeDtypeStruct((1, C), F32),
    )
    outs = pl.pallas_call(
        kernel,
        out_shape=shapes,
        in_specs=[anywhere, anywhere, vm, vm, vm, vm, anywhere],
        out_specs=(anywhere, anywhere, vm, vm, vm),
        scratch_shapes=scratch(),
        compiler_params=pltpu.CompilerParams(
            collective_id=0, has_side_effects=True, vmem_limit_bytes=60 * 1024 * 1024
        ),
    )(slab, pair, pair_mask, wt, w_out, w_bias.T, d_out)
    in_hbm = pl.BlockSpec(memory_space=pltpu.HBM)
    d_slab, d_pair, dw, dwout, dwb = pl.pallas_call(
        hand_on,
        out_shape=shapes,
        in_specs=[in_hbm] * 5,
        out_specs=(in_hbm,) * 5,
        scratch_shapes=[pltpu.VMEM(one.shape, one.dtype) for one in shapes]
        + [pltpu.SemaphoreType.DMA((2, 20))],
    )(*outs)
    return (
        d_slab.reshape(ROWS, N, C),
        jnp.swapaxes(d_pair, 1, 2),
        jnp.transpose(dw.reshape(4, DH, C), (2, 0, 1)),
        dwout,
        dwb.T,
    )


def solution(mesh):
    placed = (
        P("rows", None, None),
        P("rows", None, None),
        P("rows", None),
        P(None, None, "heads"),
        P("heads", None),
        P(),
        P("rows", None, None),
    )
    return jax.shard_map(
        shards,
        mesh=mesh,
        in_specs=placed,
        out_specs=(
            P("rows", None, None),
            P("rows", None, "heads"),
            P(None, None, "heads"),
            P("heads", None),
            P(None, "heads"),
        ),
        check_vma=False,
    )
```

```python
import jax
import jax.numpy as jnp
from jax import lax
from jax.experimental import pallas as pl
from jax.experimental.pallas import tpu as pltpu
from jax.sharding import PartitionSpec as P

MESH = pl.DeviceIdType.MESH
F32 = jnp.float32
BF16 = jnp.bfloat16
N = 1024
C = 128
DH = 32
ROWS = 4
OWN = 16
BLK = 256
HALF = 512
EPS = 1e-05
SCALE = 1.0 / DH**0.5


def nn(a, b):
    return lax.dot_general(a, b, (((1,), (0,)), ((), ())), preferred_element_type=F32)


def nt(a, b):
    return lax.dot_general(a, b, (((1,), (1,)), ((), ())), preferred_element_type=F32)


def norm_cols(t):
    cen = t - jnp.mean(t, axis=0, keepdims=True)
    r = lax.rsqrt(jnp.mean(cen * cen, axis=0, keepdims=True) + EPS)
    return cen * r, r


class Sems:
    def __init__(self):
        self.count = 0

    def take(self, n):
        first = self.count
        self.count += n
        return first


SEMS = Sems()
G1 = SEMS.take(1)
GP = SEMS.take(32)
GC = SEMS.take(2)
R1 = SEMS.take(2)
R2 = SEMS.take(16)
R3 = SEMS.take(16)
R4 = SEMS.take(8)
S1 = SEMS.take(8)
S2 = SEMS.take(4)
T1 = SEMS.take(8)
T2 = SEMS.take(4)
W1 = SEMS.take(8)
W2 = SEMS.take(8)
W3 = SEMS.take(8)
B1 = SEMS.take(8)
B2 = SEMS.take(8)
LOW = slice(0, HALF)
HIGH = slice(HALF, N)


def kernel(
    slab_h, pair_h, mask, wt, wout, wbias, dout_h,
    o_dslab, o_dpair, o_dw, o_dwout, o_dwb,
    slab, pair, dout, wn, wbt, wb,
    plane, dbias, xpt, braw, yq, rp, own_bias, ys, rs, xst, zq, z, rhs, natt,
    dkv, gate_s, do_s, s1, r1, s2, r2a, r2b, s3, r3a, r3b, s4, r4, dball,
    dxs, e1, dxc, e2, dsl, dpair, wacc, w1r, wpart, w2r, wtot, fold, bsum, b1r, b2r,
    send, recv, load,
):
    r = lax.axis_index("rows")
    h = lax.axis_index("heads")
    c = lax.rem(r, 2)
    x = lax.rem(r // 2, 4)
    zh = lax.rem(r // 8, 2)
    y = r // 16
    oz = 1 - zh
    inner = (h == 1) | (h == 2)
    at_end = jnp.logical_not(inner)
    side = h // 2
    mine = jnp.where(inner, h - 1, 0)
    to_inner = (r, jnp.where(inner, 3 - h, 1 + side))
    to_end = (r, jnp.where(h == 1, 0, 3))
    to_other = (r, 3 - h)

    def off(a, d):
        return lax.rem(a + d, 4)

    def flip(a, e):
        return 1 - a if e else a

    def peer(dy=0, ez=0, dx=0, ec=0, dh=0):
        row = ((off(y, dy) * 2 + flip(zh, ez)) * 4 + off(x, dx)) * 2 + flip(c, ec)
        return (row, off(h, dh))

    def copy(src, dst, sem, to):
        return pltpu.make_async_remote_copy(
            src_ref=src, dst_ref=dst, send_sem=send.at[sem], recv_sem=recv.at[sem],
            device_id=to, device_id_type=MESH,
        )

    loads = [pltpu.make_async_copy(pair_h.at[4 * k : 4 * k + 4], pair.at[4 * k : 4 * k + 4], load.at[k]) for k in range(4)]
    loads.append(pltpu.make_async_copy(slab_h, slab, load.at[4]))
    loads.append(pltpu.make_async_copy(dout_h, dout, load.at[5]))
    for cp in loads:
        cp.start()

    near = [(dx, ec) for dx in range(4) for ec in range(2) if dx or ec]
    far = [(dy, ez) for dy in range(4) for ez in range(2) if dy or ez]
    peers = [peer(dx=a, ec=b) for a, b in near] + [peer(dy=a, ez=b) for a, b in far]
    for d in (1, 2, 3):
        peers += [peer(dh=d), peer(ez=1, dh=d)]
    barrier = pltpu.get_barrier_semaphore()
    for to in peers:
        pl.semaphore_signal(barrier, inc=1, device_id=to, device_id_type=MESH)

    eye = (
        lax.broadcasted_iota(jnp.int32, (C, C), 0) == lax.broadcasted_iota(jnp.int32, (C, C), 1)
    ).astype(F32).astype(BF16)

    wn[...] = nt(eye, wt[...]).astype(BF16)
    row16 = lax.broadcasted_iota(jnp.int32, (16, C), 0)
    heads = wbias[...].astype(F32)
    wrel = jnp.zeros((16, C), F32)
    for k in range(4):
        wrel = wrel + jnp.where(row16 == off(h + 4, -k), heads[k : k + 1, :], 0.0)
    wb[...] = wrel.astype(BF16)
    wbt[...] = nt(eye, wrel.astype(BF16))
    wbar = jnp.mean(wrel, axis=1, keepdims=True)

    def pair_row(j, _):
        yt, rj = norm_cols(nt(eye, pair[j]))
        xb = yt.astype(BF16)
        xpt[j] = xb
        rp[pl.ds(j, 1), :] = rj
        ys[lax.rem(j, 2)] = yt
        yq[j] = ys[lax.rem(j, 2), pl.ds(pl.multiple_of(h * DH, DH), DH), :]
        raw = nn(wb[...], xb)
        braw[j] = raw
        own_bias[pl.ds(j, 1), :] = raw[0:1, :]
        return 0

    for k in range(4):
        loads[k].wait()
        lax.fori_loop(4 * k, 4 * k + 4, pair_row, 0, unroll=True)
    plane[y, zh, x, c] = own_bias[...].astype(BF16)
    pl.semaphore_wait(barrier, len(peers))

    def gather_first(s):
        zs = flip(zh, s)
        out = []
        for d in (1, 2, 3):
            low = plane.at[y, zs, x, c, :, LOW]
            high = plane.at[y, zs, x, c, :, HIGH]
            out.append(copy(low, low, GP + 16 * s + d, peer(dx=d)))
            out.append(copy(high, high, GP + 16 * s + 4 + d, peer(dy=d)))
        return out

    def gather_second(s):
        zs = flip(zh, s)
        out = []
        for d in (1, 2, 3):
            low = plane.at[y, zs, :, c, :, LOW]
            high = plane.at[:, zs, x, c, :, HIGH]
            out.append(copy(low, low, GP + 16 * s + 8 + d, peer(dy=d)))
            out.append(copy(high, high, GP + 16 * s + 12 + d, peer(dx=d)))
        return out

    def gather_core(s):
        zs = flip(zh, s)
        return copy(plane.at[:, zs, :, c], plane.at[:, zs, :, c], GC + s, peer(ec=1))

    def begin(copies):
        for cp in copies:
            cp.start()

    def end(copies):
        for cp in copies:
            cp.wait()

    g1 = copy(plane.at[y, zh, x, c], plane.at[y, zh, x, c], G1, peer(ez=1))
    g1.start()
    ga1 = gather_first(0)
    begin(ga1)

    def slab_row(i, _):
        yt, ri = norm_cols(nt(eye, slab[i]))
        ys[i] = yt
        rs[pl.ds(i, 1), :] = ri
        xb = yt.astype(BF16)
        xst[i] = xb
        proj = nn(wt[...], xb)
        gate = 1.0 / (1.0 + jnp.exp(-proj[96:128]))
        do = nt(wout[...], dout[i])
        gate_s[i] = gate
        do_s[i] = do
        datt = do * gate
        stack = jnp.concatenate([proj[0:96], datt], axis=0)
        z[i] = stack.T.astype(BF16).reshape(4, 2, 128, C)
        both = jnp.concatenate([proj[0:DH], datt], axis=0).astype(BF16)
        for k in range(8):
            zq[i, k] = both[:, k * 128 : (k + 1) * 128]
        rhs[i, 0:DH, 0:N] = proj[32:64].astype(BF16)
        rhs[i, 96:128, N : 2 * N] = proj[64:96].astype(BF16)
        return 0

    rhs[...] = jnp.zeros(rhs.shape, BF16)
    loads[4].wait()
    loads[5].wait()
    lax.fori_loop(0, 2, slab_row, 0)
    end(ga1)
    ga2 = gather_second(0)
    begin(ga2)
    g1.wait()
    gb1 = gather_first(1)
    begin(gb1)
    lax.fori_loop(2, ROWS, slab_row, 0)
    wacc[...] = jnp.zeros(wacc.shape, F32)
    dkv[...] = jnp.zeros(dkv.shape, F32)
    dbias[...] = jnp.zeros(dbias.shape, F32)
    end(gb1)
    gb2 = gather_second(1)
    begin(gb2)
    end(ga2)
    gac = gather_core(0)
    gac.start()
    gac.wait()

    def block(i, yy, zs):
        keep = mask[pl.ds(i, 1), :] == 1
        two = pl.ds(2 * yy, 2)
        zj = z[i, two, zs].reshape(BLK, C)
        bias = plane[two, zs].reshape(BLK, N).astype(F32)
        logits = nn(zj[:, 0:DH], rhs[i, 0:DH, 0:N]) * SCALE + bias
        logits = jnp.where(keep, logits, -1e9)
        expo = jnp.exp(logits - jnp.max(logits, axis=1, keepdims=True))
        probs = expo * (1.0 / jnp.sum(expo, axis=1, keepdims=True))
        pb = probs.astype(BF16)
        dp = nn(zj[:, 96:128], rhs[i, 96:128, N : 2 * N])
        dl = probs * (dp - jnp.sum(probs * dp, axis=1, keepdims=True))
        dl = jnp.where(keep, dl, 0.0)
        dlb = dl.astype(BF16)
        dbias[two, zs] += dl.reshape(2, 4, 2, OWN, N)
        zall = z[i].reshape(N, C)
        lane = lax.broadcasted_iota(jnp.int32, (BLK, C), 1)
        nat = jnp.where(lane < 64, nn(dlb, zall), nn(pb, zall))
        natt[i, two, zs] = nat.reshape(2, 128, C)
        left = jnp.concatenate([zq[i, 4 * yy + zs], zq[i, 4 * yy + 2 + zs]], axis=1)
        dkv[i, 0:DH, :] += nn(left[0:DH], dlb)
        dkv[i, DH:64, :] += nn(left[DH:64], pb)

    def own_half(t, _):
        block(t // 2, lax.rem(t, 2), zh)
        return 0

    def other_half(t, _):
        block(t // 2, lax.rem(t, 2), oz)
        return 0

    def up_copies(i):
        far_half = 1 - side
        return [
            copy(dxs.at[i, far_half], e1.at[i, far_half], S1 + 2 * i, to_inner),
            copy(dxs.at[i, side], e1.at[i, side], S1 + 2 * i + 1, to_inner),
        ]

    def cross_copy(i):
        return copy(dxc.at[i], e2.at[i], S2 + i, to_other)

    def done_copies(i):
        return [
            copy(dsl.at[i, mine], dsl.at[i, mine], T1 + 2 * i, to_other),
            copy(dsl.at[i, mine], dsl.at[i, mine], T1 + 2 * i + 1, to_end),
        ]

    def pass_copy(i):
        return copy(dsl.at[i, 1 - mine], dsl.at[i, 1 - mine], T2 + i, to_end)

    def send_row(i):
        @pl.when(at_end)
        def _():
            begin(up_copies(i))

    def middle_slab(i):
        @pl.when(inner)
        def _():
            up_copies(i)[0].wait_recv()
            g = dxs[i, 1 - mine].astype(F32) + e1[i, 1 - mine].astype(F32)
            dxc[i] = g.astype(BF16)
            cross_copy(i).start()

    def finish_slab(i):
        @pl.when(inner)
        def _():
            up_copies(i)[1].wait_recv()
            cross_copy(i).wait()
            g = dxs[i, mine].astype(F32) + e1[i, mine].astype(F32) + e2[i].astype(F32)
            cols = pl.ds(pl.multiple_of(mine * HALF, HALF), HALF)
            yt = ys[i, :, cols]
            ri = rs[pl.ds(i, 1), cols]
            first = jnp.mean(g, axis=0, keepdims=True)
            out = ri * (g - first - yt * jnp.mean(g * yt, axis=0, keepdims=True))
            dsl[i, mine] = out.T.astype(BF16)
            begin(done_copies(i))

    def pass_slab(i):
        @pl.when(inner)
        def _():
            done_copies(i)[0].wait_recv()
            pass_copy(i).start()

    def end_slab(i):
        @pl.when(inner)
        def _():
            for cp in done_copies(i) + [pass_copy(i)]:
                cp.wait_send()

        @pl.when(at_end)
        def _():
            for cp in up_copies(i):
                cp.wait_send()
            done_copies(i)[1].wait_recv()
            pass_copy(i).wait_recv()

    def finish_row(i):
        nat = natt[i].reshape(N, C).T
        gate = gate_s[i]
        do = do_s[i]
        att = nat[64:96]
        gated = (gate * att).astype(BF16)
        dgate = do * att * gate * (1.0 - gate)
        grads = jnp.concatenate(
            [nat[32:64] * SCALE, dkv[i, 0:DH, :] * SCALE, dkv[i, DH:64, :], dgate], axis=0
        ).astype(BF16)
        dx = nn(wn[...], grads).astype(BF16)
        dxs[i, 0] = dx[:, LOW]
        dxs[i, 1] = dx[:, HIGH]
        send_row(i)
        wacc[0:C, :] += nt(grads, xst[i])
        wacc[C : C + DH, :] += nn(gated, dout[i])

    def sum_core(s):
        zs = flip(zh, s)
        s1[s] = dbias[:, zs, :, 1 - c].astype(BF16)
        return copy(s1.at[s], r1.at[s], R1 + s, peer(ec=1))

    def sum_first(s):
        zs = flip(zh, s)
        for yy in range(4):
            total = dbias[yy, zs, :, c] + r1[s, yy].astype(F32)
            dbias[yy, zs, :, c] = total
            s2[s, yy] = total.astype(BF16)
        out = []
        for d in (1, 2, 3):
            low = s2.at[s, off(y, d), :, :, LOW]
            high = s2.at[s, :, off(x, d), :, HIGH]
            out.append(copy(low, r2a.at[s, d], R2 + 8 * s + d, peer(dy=d)))
            out.append(copy(high, r2b.at[s, d], R2 + 8 * s + 4 + d, peer(dx=d)))
        return out

    def sum_second(s):
        zs = flip(zh, s)
        low = dbias[y, zs, :, c, :, LOW]
        high = dbias[:, zs, x, c, :, HIGH]
        for d in (1, 2, 3):
            low = low + r2a[s, d].astype(F32)
            high = high + r2b[s, d].astype(F32)
        s3[s, 0] = low.astype(BF16)
        s3[s, 1] = high.astype(BF16)
        dbias[y, zs, :, c, :, LOW] = low
        dbias[:, zs, x, c, :, HIGH] = high
        out = []
        for d in (1, 2, 3):
            out.append(copy(s3.at[s, 0, off(x, d)], r3a.at[s, d], R3 + 8 * s + d, peer(dx=d)))
            out.append(copy(s3.at[s, 1, off(y, d)], r3b.at[s, d], R3 + 8 * s + 4 + d, peer(dy=d)))
        return out

    def sum_last(s):
        zs = flip(zh, s)
        low = dbias[y, zs, x, c, :, LOW]
        high = dbias[y, zs, x, c, :, HIGH]
        for d in (1, 2, 3):
            low = low + r3a[s, d].astype(F32)
            high = high + r3b[s, d].astype(F32)
        both = jnp.concatenate([low, high], axis=1)
        s4[s] = both.astype(BF16)
        out = []
        for d in range(4):
            if s or d:
                out.append(copy(s4.at[s], r4.at[s, d], R4 + 4 * s + d, peer(ez=s, dh=d)))
        return both, out

    def own_row(i):
        lax.fori_loop(2 * i, 2 * i + 2, own_half, 0, unroll=2)

    def other_row(i):
        lax.fori_loop(2 * i, 2 * i + 2, other_half, 0, unroll=2)

    lax.fori_loop(0, 4, own_half, 0, unroll=2)
    end(gb2)
    gbc = gather_core(1)
    gbc.start()
    gbc.wait()
    for i in range(2):
        other_row(i)
        finish_row(i)
    own_row(2)
    middle_slab(0)
    other_row(2)
    finish_row(2)
    middle_slab(1)
    own_row(3)
    ra1 = sum_core(0)
    ra1.start()
    finish_slab(0)
    other_row(3)
    rb1 = sum_core(1)
    rb1.start()
    finish_row(3)
    chunk = 24

    def wslice(k):
        return pl.ds(pl.multiple_of(k * chunk, 8), chunk)

    def wid(dx, ec):
        return off(x, dx) * 2 + flip(c, ec)

    w1 = [
        copy(wacc.at[wslice(wid(a, b))], w1r.at[2 * a + b], W1 + 2 * a + b, peer(dx=a, ec=b))
        for a, b in near
    ]
    rb1.wait()
    rb2 = sum_first(1)
    begin(rb2)
    begin(w1)
    finish_slab(1)
    pass_slab(0)
    middle_slab(2)
    ra1.wait()
    ra2 = sum_first(0)
    end(rb2)
    rb3 = sum_second(1)
    begin(rb3)
    begin(ra2)
    pass_slab(1)
    finish_slab(2)
    end(w1)
    part = wacc[wslice(wid(0, 0)), :]
    for a, b in near:
        part = part + w1r[2 * a + b]
    wpart[...] = part
    w2 = [copy(wpart, w2r.at[2 * a + b], W2 + 2 * a + b, peer(dy=a, ez=b)) for a, b in far]
    begin(w2)
    middle_slab(3)
    end(rb3)
    _, rb4 = sum_last(1)
    begin(rb4)
    end(ra2)
    ra3 = sum_second(0)
    begin(ra3)
    pass_slab(2)
    finish_slab(3)
    end(ra3)
    own, ra4 = sum_last(0)
    begin(ra4)
    rb4[0].wait()

    db = own + r4[1, 0].astype(F32)
    own_bias[...] = db
    dball[:, 0, :] = db

    def wb_part(k, _):
        sub = pl.ds(pl.multiple_of(k * 32, 32), 32)
        acc = xpt[0, sub, :].astype(F32) * own_bias[0:1, :]
        for j in range(1, OWN):
            acc = acc + xpt[j, sub, :].astype(F32) * own_bias[j : j + 1, :]
        total = acc[:, 0:128]
        for q in range(1, 8):
            total = total + acc[:, q * 128 : (q + 1) * 128]
        fold[sub, :] = total
        return 0

    lax.fori_loop(0, 4, wb_part, 0)
    total = fold[...]
    hi = total.astype(BF16)
    mid = (total - hi.astype(F32)).astype(BF16)
    lo = (total - hi.astype(F32) - mid.astype(F32)).astype(BF16)
    ones = jnp.ones((16, C), F32).astype(BF16)
    bsum[0] = (nt(ones, hi) + nt(ones, mid) + nt(ones, lo))[0:8]
    b1 = [copy(bsum.at[0], b1r.at[2 * a + b], B1 + 2 * a + b, peer(dx=a, ec=b)) for a, b in near]
    begin(b1)
    end(w2)
    part = wpart[...]
    for a, b in far:
        part = part + w2r[2 * a + b]
    wtot[wslice(wid(0, 0)), :] = part
    w3 = [
        copy(
            wtot.at[wslice(wid(0, 0))], wtot.at[wslice(wid(0, 0))], W3 + 2 * a + b,
            peer(dx=a, ec=b),
        )
        for a, b in near
    ]
    begin(w3)

    def dpair_row(j, _):
        dbj = dball[j]
        wq = wbt[pl.ds(pl.multiple_of(h * DH, DH), DH), :].astype(BF16)
        g = nn(wq, dbj.astype(BF16))
        first = jnp.sum(dbj * wbar, axis=0, keepdims=True)
        second = jnp.sum(dbj * braw[j], axis=0, keepdims=True) * (1.0 / C)
        dpair[j] = (rp[pl.ds(j, 1), :] * (g - first - yq[j] * second)).astype(BF16)
        return 0

    end(ra4)
    end(rb4[1:])
    pass_slab(3)
    for d in (1, 2, 3):
        dball[:, d, :] = r4[0, d].astype(F32) + r4[1, d].astype(F32)
    dball[:, 4:16, :] = jnp.zeros((OWN, 12, N), F32)
    lax.fori_loop(0, 8, dpair_row, 0, unroll=4)
    out_low = pltpu.make_async_copy(dpair.at[0:8], o_dpair.at[0:8], load.at[4])
    out_low.start()
    end(b1)
    part = bsum[0]
    for a, b in near:
        part = part + b1r[2 * a + b]
    bsum[1] = part
    b2 = [copy(bsum.at[1], b2r.at[2 * a + b], B2 + 2 * a + b, peer(dy=a, ez=b)) for a, b in far]
    begin(b2)
    lax.fori_loop(8, OWN, dpair_row, 0, unroll=4)
    out_high = pltpu.make_async_copy(dpair.at[8:16], o_dpair.at[8:16], load.at[5])
    out_high.start()
    end(w3)
    o_dw[...] = wtot[0:C, :]
    o_dwout[...] = wtot[C : C + DH, :]
    slab_out = [pltpu.make_async_copy(dsl.at[i], o_dslab.at[i], load.at[i]) for i in range(ROWS)]
    for i in range(ROWS):
        end_slab(i)
        slab_out[i].start()
    end(b2)
    part = bsum[1]
    for a, b in far:
        part = part + b2r[2 * a + b]
    o_dwb[...] = part[0:1, :]
    for cp in slab_out + [out_low, out_high]:
        cp.wait()


def scratch():
    v = pltpu.VMEM
    return [
        v((ROWS, N, C), BF16),
        v((OWN, N, C), BF16),
        v((ROWS, N, C), BF16),
        v((C, C), BF16),
        v((C, 16), F32),
        v((16, C), BF16),
        v((4, 2, 4, 2, OWN, N), BF16),
        v((4, 2, 4, 2, OWN, N), F32),
        v((OWN, C, N), BF16),
        v((OWN, OWN, N), F32),
        v((OWN, DH, N), F32),
        v((OWN, N), F32),
        v((OWN, N), F32),
        v((ROWS, C, N), F32),
        v((8, N), F32),
        v((ROWS, C, N), BF16),
        v((ROWS, 8, 64, 128), BF16),
        v((ROWS, 4, 2, 128, C), BF16),
        v((ROWS, C, 2 * N), BF16),
        v((ROWS, 4, 2, 128, C), F32),
        v((ROWS, 64, N), F32),
        v((ROWS, DH, N), F32),
        v((ROWS, DH, N), F32),
        v((2, 4, 4, OWN, N), BF16),
        v((2, 4, 4, OWN, N), BF16),
        v((2, 4, 4, OWN, N), BF16),
        v((2, 4, 4, OWN, HALF), BF16),
        v((2, 4, 4, OWN, HALF), BF16),
        v((2, 2, 4, OWN, HALF), BF16),
        v((2, 4, OWN, HALF), BF16),
        v((2, 4, OWN, HALF), BF16),
        v((2, OWN, N), BF16),
        v((2, 4, OWN, N), BF16),
        v((OWN, OWN, N), F32),
        v((ROWS, 2, C, HALF), BF16),
        v((ROWS, 2, C, HALF), BF16),
        v((ROWS, C, HALF), BF16),
        v((ROWS, C, HALF), BF16),
        v((ROWS, 2, HALF, C), BF16),
        v((OWN, DH, N), BF16),
        v((192, C), F32),
        v((8, 24, C), F32),
        v((24, C), F32),
        v((8, 24, C), F32),
        v((192, C), F32),
        v((C, C), F32),
        v((2, 8, C), F32),
        v((8, 8, C), F32),
        v((8, 8, C), F32),
        pltpu.SemaphoreType.DMA((SEMS.count,)),
        pltpu.SemaphoreType.DMA((SEMS.count,)),
        pltpu.SemaphoreType.DMA((6,)),
    ]


def hand_on(*refs):
    outs, held, sem = refs[5:10], refs[10:15], refs[15]
    first, second = [], []
    for k in range(5):
        pieces = 4 if k < 2 else 1
        for q in range(pieces):
            size = held[k].shape[0] // pieces
            part = pl.ds(q * size, size)
            one = sem.at[0, 4 * k + q]
            two = sem.at[1, 4 * k + q]
            first.append(pltpu.make_async_copy(refs[k].at[part], held[k].at[part], one))
            second.append(pltpu.make_async_copy(held[k].at[part], outs[k].at[part], two))
    for cp in first:
        cp.start()
    for cp, then in zip(first, second):
        cp.wait()
        then.start()
    for cp in second:
        cp.wait()


def shards(slab, pair, pair_mask, w_qkvg, w_out, w_bias, d_out):
    wt = jnp.transpose(w_qkvg, (1, 2, 0)).reshape(C, C)
    vm = pl.BlockSpec(memory_space=pltpu.VMEM)
    anywhere = pl.BlockSpec(memory_space=pl.ANY)
    shapes = (
        jax.ShapeDtypeStruct((ROWS, 2, HALF, C), BF16),
        jax.ShapeDtypeStruct((OWN, DH, N), BF16),
        jax.ShapeDtypeStruct((C, C), F32),
        jax.ShapeDtypeStruct((DH, C), F32),
        jax.ShapeDtypeStruct((1, C), F32),
    )
    outs = pl.pallas_call(
        kernel,
        out_shape=shapes,
        in_specs=[anywhere, anywhere, vm, vm, vm, vm, anywhere],
        out_specs=(anywhere, anywhere, vm, vm, vm),
        scratch_shapes=scratch(),
        compiler_params=pltpu.CompilerParams(
            collective_id=0, has_side_effects=True, vmem_limit_bytes=60 * 1024 * 1024
        ),
    )(slab, pair, pair_mask, wt, w_out, w_bias.T, d_out)
    in_hbm = pl.BlockSpec(memory_space=pltpu.HBM)
    d_slab, d_pair, dw, dwout, dwb = pl.pallas_call(
        hand_on,
        out_shape=shapes,
        in_specs=[in_hbm] * 5,
        out_specs=(in_hbm,) * 5,
        scratch_shapes=[pltpu.VMEM(one.shape, one.dtype) for one in shapes]
        + [pltpu.SemaphoreType.DMA((2, 20))],
    )(*outs)
    return (
        d_slab.reshape(ROWS, N, C),
        jnp.swapaxes(d_pair, 1, 2),
        jnp.transpose(dw.reshape(4, DH, C), (2, 0, 1)),
        dwout,
        dwb.T,
    )


def solution(mesh):
    placed = (
        P("rows", None, None),
        P("rows", None, None),
        P("rows", None),
        P(None, None, "heads"),
        P("heads", None),
        P(),
        P("rows", None, None),
    )
    return jax.shard_map(
        shards,
        mesh=mesh,
        in_specs=placed,
        out_specs=(
            P("rows", None, None),
            P("rows", None, "heads"),
            P(None, None, "heads"),
            P("heads", None),
            P(None, "heads"),
        ),
        check_vma=False,
    )
```

```python
import jax
import jax.numpy as jnp
from jax import lax
from jax.experimental import pallas as pl
from jax.experimental.pallas import tpu as pltpu
from jax.sharding import PartitionSpec as P

MESH = pl.DeviceIdType.MESH
F32 = jnp.float32
BF16 = jnp.bfloat16
N = 1024
C = 128
DH = 32
ROWS = 4
OWN = 16
BLK = 256
HALF = 512
EPS = 1e-05
SCALE = 1.0 / DH**0.5


def nn(a, b):
    return lax.dot_general(a, b, (((1,), (0,)), ((), ())), preferred_element_type=F32)


def nt(a, b):
    return lax.dot_general(a, b, (((1,), (1,)), ((), ())), preferred_element_type=F32)


def norm_cols(t):
    cen = t - jnp.mean(t, axis=0, keepdims=True)
    r = lax.rsqrt(jnp.mean(cen * cen, axis=0, keepdims=True) + EPS)
    return cen * r, r


class Sems:
    def __init__(self):
        self.count = 0

    def take(self, n):
        first = self.count
        self.count += n
        return first


SEMS = Sems()
G1 = SEMS.take(1)
GP = SEMS.take(32)
GC = SEMS.take(2)
R1 = SEMS.take(2)
R2 = SEMS.take(16)
R3 = SEMS.take(16)
R4 = SEMS.take(4)
S1 = SEMS.take(8)
S2 = SEMS.take(4)
T1 = SEMS.take(8)
T2 = SEMS.take(4)
W1 = SEMS.take(8)
W2 = SEMS.take(8)
W3 = SEMS.take(8)
B1 = SEMS.take(8)
B2 = SEMS.take(8)
LOW = slice(0, HALF)
HIGH = slice(HALF, N)


def kernel(
    slab_h, pair_h, mask, wt, wout, wbias, dout_h,
    o_dslab, o_dpair, o_dw, o_dwout, o_dwb,
    slab, pair, dout, wn, wbt, wb,
    plane, dbias, xpt, braw, yq, rp, own_bias, ys, rs, xst, zq, z, rhs, natt,
    dkv, gate_s, do_s, s1, r1, s2, r2a, r2b, s3, r3a, r3b, s4, r4, dball,
    dxs, e1, dxc, e2, dsl, dpair, wacc, w1r, wpart, w2r, wtot, fold, bsum, b1r, b2r,
    send, recv, load,
):
    r = lax.axis_index("rows")
    h = lax.axis_index("heads")
    c = lax.rem(r, 2)
    x = lax.rem(r // 2, 4)
    zh = lax.rem(r // 8, 2)
    y = r // 16
    oz = 1 - zh
    inner = (h == 1) | (h == 2)
    at_end = jnp.logical_not(inner)
    side = h // 2
    mine = jnp.where(inner, h - 1, 0)
    to_inner = (r, jnp.where(inner, 3 - h, 1 + side))
    to_end = (r, jnp.where(h == 1, 0, 3))
    to_other = (r, 3 - h)

    def off(a, d):
        return lax.rem(a + d, 4)

    def flip(a, e):
        return 1 - a if e else a

    def peer(dy=0, ez=0, dx=0, ec=0, dh=0):
        row = ((off(y, dy) * 2 + flip(zh, ez)) * 4 + off(x, dx)) * 2 + flip(c, ec)
        return (row, off(h, dh))

    def copy(src, dst, sem, to):
        return pltpu.make_async_remote_copy(
            src_ref=src, dst_ref=dst, send_sem=send.at[sem], recv_sem=recv.at[sem],
            device_id=to, device_id_type=MESH,
        )

    loads = [pltpu.make_async_copy(pair_h.at[4 * k : 4 * k + 4], pair.at[4 * k : 4 * k + 4], load.at[k]) for k in range(4)]
    loads.append(pltpu.make_async_copy(slab_h, slab, load.at[4]))
    loads.append(pltpu.make_async_copy(dout_h, dout, load.at[5]))
    for cp in loads:
        cp.start()

    near = [(dx, ec) for dx in range(4) for ec in range(2) if dx or ec]
    far = [(dy, ez) for dy in range(4) for ez in range(2) if dy or ez]
    peers = [peer(dx=a, ec=b) for a, b in near] + [peer(dy=a, ez=b) for a, b in far]
    for d in (1, 2, 3):
        peers.append(peer(dh=d))
    barrier = pltpu.get_barrier_semaphore()
    for to in peers:
        pl.semaphore_signal(barrier, inc=1, device_id=to, device_id_type=MESH)

    eye = (
        lax.broadcasted_iota(jnp.int32, (C, C), 0) == lax.broadcasted_iota(jnp.int32, (C, C), 1)
    ).astype(F32).astype(BF16)

    wn[...] = nt(eye, wt[...]).astype(BF16)
    row16 = lax.broadcasted_iota(jnp.int32, (16, C), 0)
    heads = wbias[...].astype(F32)
    wrel = jnp.zeros((16, C), F32)
    for k in range(4):
        wrel = wrel + jnp.where(row16 == off(h + 4, -k), heads[k : k + 1, :], 0.0)
    wb[...] = wrel.astype(BF16)
    wbt[...] = nt(eye, wrel.astype(BF16))
    wbar = jnp.mean(wrel, axis=1, keepdims=True)

    def pair_row(j, _):
        yt, rj = norm_cols(nt(eye, pair[j]))
        xb = yt.astype(BF16)
        xpt[j] = xb
        rp[pl.ds(j, 1), :] = rj
        ys[lax.rem(j, 2)] = yt
        yq[j] = ys[lax.rem(j, 2), pl.ds(pl.multiple_of(h * DH, DH), DH), :]
        raw = nn(wb[...], xb)
        braw[j] = raw
        own_bias[pl.ds(j, 1), :] = raw[0:1, :]
        return 0

    for k in range(4):
        loads[k].wait()
        lax.fori_loop(4 * k, 4 * k + 4, pair_row, 0, unroll=True)
    plane[y, zh, x, c] = own_bias[...].astype(BF16)
    pl.semaphore_wait(barrier, len(peers))

    def gather_first(s):
        zs = flip(zh, s)
        out = []
        for d in (1, 2, 3):
            low = plane.at[y, zs, x, c, :, LOW]
            high = plane.at[y, zs, x, c, :, HIGH]
            out.append(copy(low, low, GP + 16 * s + d, peer(dx=d)))
            out.append(copy(high, high, GP + 16 * s + 4 + d, peer(dy=d)))
        return out

    def gather_second(s):
        zs = flip(zh, s)
        out = []
        for d in (1, 2, 3):
            low = plane.at[y, zs, :, c, :, LOW]
            high = plane.at[:, zs, x, c, :, HIGH]
            out.append(copy(low, low, GP + 16 * s + 8 + d, peer(dy=d)))
            out.append(copy(high, high, GP + 16 * s + 12 + d, peer(dx=d)))
        return out

    def gather_core(s):
        zs = flip(zh, s)
        return copy(plane.at[:, zs, :, c], plane.at[:, zs, :, c], GC + s, peer(ec=1))

    def begin(copies):
        for cp in copies:
            cp.start()

    def end(copies):
        for cp in copies:
            cp.wait()

    g1 = copy(plane.at[y, zh, x, c], plane.at[y, zh, x, c], G1, peer(ez=1))
    g1.start()
    ga1 = gather_first(0)
    begin(ga1)

    def slab_row(i, _):
        yt, ri = norm_cols(nt(eye, slab[i]))
        ys[i] = yt
        rs[pl.ds(i, 1), :] = ri
        xb = yt.astype(BF16)
        xst[i] = xb
        proj = nn(wt[...], xb)
        gate = 1.0 / (1.0 + jnp.exp(-proj[96:128]))
        do = nt(wout[...], dout[i])
        gate_s[i] = gate
        do_s[i] = do
        datt = do * gate
        stack = jnp.concatenate([proj[0:96], datt], axis=0)
        z[i] = stack.T.astype(BF16).reshape(4, 2, 128, C)
        both = jnp.concatenate([proj[0:DH], datt], axis=0).astype(BF16)
        for k in range(8):
            zq[i, k] = both[:, k * 128 : (k + 1) * 128]
        rhs[i, 0:DH, 0:N] = proj[32:64].astype(BF16)
        rhs[i, 96:128, N : 2 * N] = proj[64:96].astype(BF16)
        return 0

    rhs[...] = jnp.zeros(rhs.shape, BF16)
    loads[4].wait()
    loads[5].wait()
    lax.fori_loop(0, 2, slab_row, 0)
    end(ga1)
    ga2 = gather_second(0)
    begin(ga2)
    g1.wait()
    gb1 = gather_first(1)
    begin(gb1)
    lax.fori_loop(2, ROWS, slab_row, 0)
    wacc[...] = jnp.zeros(wacc.shape, F32)
    dkv[...] = jnp.zeros(dkv.shape, F32)
    dbias[...] = jnp.zeros(dbias.shape, F32)
    end(gb1)
    gb2 = gather_second(1)
    begin(gb2)
    end(ga2)
    gac = gather_core(0)
    gac.start()
    gac.wait()

    def block(i, zs):
        keep = mask[pl.ds(i, 1), :] == 1
        zj = z[i, :, zs].reshape(HALF, C)
        bias = plane[:, zs].reshape(HALF, N).astype(F32)
        logits = nn(zj[:, 0:DH], rhs[i, 0:DH, 0:N]) * SCALE + bias
        logits = jnp.where(keep, logits, -1e9)
        expo = jnp.exp(logits - jnp.max(logits, axis=1, keepdims=True))
        probs = expo * (1.0 / jnp.sum(expo, axis=1, keepdims=True))
        pb = probs.astype(BF16)
        dp = nn(zj[:, 96:128], rhs[i, 96:128, N : 2 * N])
        dl = probs * (dp - jnp.sum(probs * dp, axis=1, keepdims=True))
        dl = jnp.where(keep, dl, 0.0)
        dlb = dl.astype(BF16)
        dbias[:, zs] += dl.reshape(4, 4, 2, OWN, N)
        zall = z[i].reshape(N, C)
        lane = lax.broadcasted_iota(jnp.int32, (HALF, C), 1)
        nat = jnp.where(lane < 64, nn(dlb, zall), nn(pb, zall))
        natt[i, :, zs] = nat.reshape(4, 128, C)
        left = jnp.concatenate([zq[i, 2 * k + zs] for k in range(4)], axis=1)
        dkv[i, 0:DH, :] += nn(left[0:DH], dlb)
        dkv[i, DH:64, :] += nn(left[DH:64], pb)

    def up_copies(i):
        far_half = 1 - side
        return [
            copy(dxs.at[i, far_half], e1.at[i, far_half], S1 + 2 * i, to_inner),
            copy(dxs.at[i, side], e1.at[i, side], S1 + 2 * i + 1, to_inner),
        ]

    def cross_copy(i):
        return copy(dxc.at[i], e2.at[i], S2 + i, to_other)

    def done_copies(i):
        return [
            copy(dsl.at[i, mine], dsl.at[i, mine], T1 + 2 * i, to_other),
            copy(dsl.at[i, mine], dsl.at[i, mine], T1 + 2 * i + 1, to_end),
        ]

    def pass_copy(i):
        return copy(dsl.at[i, 1 - mine], dsl.at[i, 1 - mine], T2 + i, to_end)

    def send_row(i):
        @pl.when(at_end)
        def _():
            begin(up_copies(i))

    def middle_slab(i):
        @pl.when(inner)
        def _():
            up_copies(i)[0].wait_recv()
            g = dxs[i, 1 - mine].astype(F32) + e1[i, 1 - mine].astype(F32)
            dxc[i] = g.astype(BF16)
            cross_copy(i).start()

    def finish_slab(i):
        @pl.when(inner)
        def _():
            up_copies(i)[1].wait_recv()
            cross_copy(i).wait()
            g = dxs[i, mine].astype(F32) + e1[i, mine].astype(F32) + e2[i].astype(F32)
            cols = pl.ds(pl.multiple_of(mine * HALF, HALF), HALF)
            yt = ys[i, :, cols]
            ri = rs[pl.ds(i, 1), cols]
            first = jnp.mean(g, axis=0, keepdims=True)
            out = ri * (g - first - yt * jnp.mean(g * yt, axis=0, keepdims=True))
            dsl[i, mine] = out.T.astype(BF16)
            begin(done_copies(i))

    def pass_slab(i):
        @pl.when(inner)
        def _():
            done_copies(i)[0].wait_recv()
            pass_copy(i).start()

    def end_slab(i):
        @pl.when(inner)
        def _():
            for cp in done_copies(i) + [pass_copy(i)]:
                cp.wait_send()

        @pl.when(at_end)
        def _():
            for cp in up_copies(i):
                cp.wait_send()
            done_copies(i)[1].wait_recv()
            pass_copy(i).wait_recv()

    def finish_row(i):
        nat = natt[i].reshape(N, C).T
        gate = gate_s[i]
        do = do_s[i]
        att = nat[64:96]
        gated = (gate * att).astype(BF16)
        dgate = do * att * gate * (1.0 - gate)
        grads = jnp.concatenate(
            [nat[32:64] * SCALE, dkv[i, 0:DH, :] * SCALE, dkv[i, DH:64, :], dgate], axis=0
        ).astype(BF16)
        dx = nn(wn[...], grads).astype(BF16)
        dxs[i, 0] = dx[:, LOW]
        dxs[i, 1] = dx[:, HIGH]
        send_row(i)
        wacc[0:C, :] += nt(grads, xst[i])
        wacc[C : C + DH, :] += nn(gated, dout[i])

    def sum_core(s):
        zs = flip(zh, s)
        s1[s] = dbias[:, zs, :, 1 - c].astype(BF16)
        return copy(s1.at[s], r1.at[s], R1 + s, peer(ec=1))

    def sum_first(s):
        zs = flip(zh, s)
        for yy in range(4):
            total = dbias[yy, zs, :, c] + r1[s, yy].astype(F32)
            dbias[yy, zs, :, c] = total
            s2[s, yy] = total.astype(BF16)
        out = []
        for d in (1, 2, 3):
            low = s2.at[s, off(y, d), :, :, LOW]
            high = s2.at[s, :, off(x, d), :, HIGH]
            out.append(copy(low, r2a.at[s, d], R2 + 8 * s + d, peer(dy=d)))
            out.append(copy(high, r2b.at[s, d], R2 + 8 * s + 4 + d, peer(dx=d)))
        return out

    def sum_second(s):
        zs = flip(zh, s)
        low = dbias[y, zs, :, c, :, LOW]
        high = dbias[:, zs, x, c, :, HIGH]
        for d in (1, 2, 3):
            low = low + r2a[s, d].astype(F32)
            high = high + r2b[s, d].astype(F32)
        s3[s, 0] = low.astype(BF16)
        s3[s, 1] = high.astype(BF16)
        dbias[y, zs, :, c, :, LOW] = low
        dbias[:, zs, x, c, :, HIGH] = high
        out = []
        for d in (1, 2, 3):
            out.append(copy(s3.at[s, 0, off(x, d)], r3a.at[s, d], R3 + 8 * s + d, peer(dx=d)))
            out.append(copy(s3.at[s, 1, off(y, d)], r3b.at[s, d], R3 + 8 * s + 4 + d, peer(dy=d)))
        return out

    def sum_last(s):
        zs = flip(zh, s)
        low = dbias[y, zs, x, c, :, LOW]
        high = dbias[y, zs, x, c, :, HIGH]
        for d in (1, 2, 3):
            low = low + r3a[s, d].astype(F32)
            high = high + r3b[s, d].astype(F32)
        return jnp.concatenate([low, high], axis=1)

    def own_row(i):
        block(i, zh)

    def other_row(i):
        block(i, oz)

    own_row(0)
    own_row(1)
    end(gb2)
    gbc = gather_core(1)
    gbc.start()
    own_row(2)
    gbc.wait()
    for i in range(3):
        other_row(i)
        finish_row(i)
    own_row(3)
    ra1 = sum_core(0)
    ra1.start()
    middle_slab(0)
    other_row(3)
    rb1 = sum_core(1)
    rb1.start()
    finish_row(3)
    chunk = 24

    def wslice(k):
        return pl.ds(pl.multiple_of(k * chunk, 8), chunk)

    def wid(dx, ec):
        return off(x, dx) * 2 + flip(c, ec)

    w1 = [
        copy(wacc.at[wslice(wid(a, b))], w1r.at[2 * a + b], W1 + 2 * a + b, peer(dx=a, ec=b))
        for a, b in near
    ]
    rb1.wait()
    rb2 = sum_first(1)
    begin(rb2)
    begin(w1)
    middle_slab(1)
    finish_slab(0)
    ra1.wait()
    ra2 = sum_first(0)
    end(rb2)
    rb3 = sum_second(1)
    begin(rb3)
    begin(ra2)
    middle_slab(2)
    finish_slab(1)
    pass_slab(0)
    end(w1)
    part = wacc[wslice(wid(0, 0)), :]
    for a, b in near:
        part = part + w1r[2 * a + b]
    wpart[...] = part
    w2 = [copy(wpart, w2r.at[2 * a + b], W2 + 2 * a + b, peer(dy=a, ez=b)) for a, b in far]
    begin(w2)
    end(rb3)
    s4[1] = sum_last(1).astype(BF16)
    rb4 = copy(s4.at[1], r4.at[0], R4, peer(ez=1))
    rb4.start()
    middle_slab(3)
    finish_slab(2)
    pass_slab(1)
    end(ra2)
    ra3 = sum_second(0)
    begin(ra3)
    finish_slab(3)
    end(ra3)
    own = sum_last(0)
    rb4.wait()

    db = own + r4[0].astype(F32)
    s4[0] = db.astype(BF16)
    r5 = [copy(s4.at[0], r4.at[d], R4 + d, peer(dh=d)) for d in (1, 2, 3)]
    begin(r5)
    own_bias[...] = db
    dball[:, 0, :] = db

    def wb_part(k, _):
        sub = pl.ds(pl.multiple_of(k * 32, 32), 32)
        acc = xpt[0, sub, :].astype(F32) * own_bias[0:1, :]
        for j in range(1, OWN):
            acc = acc + xpt[j, sub, :].astype(F32) * own_bias[j : j + 1, :]
        total = acc[:, 0:128]
        for q in range(1, 8):
            total = total + acc[:, q * 128 : (q + 1) * 128]
        fold[sub, :] = total
        return 0

    lax.fori_loop(0, 4, wb_part, 0)
    total = fold[...]
    hi = total.astype(BF16)
    mid = (total - hi.astype(F32)).astype(BF16)
    lo = (total - hi.astype(F32) - mid.astype(F32)).astype(BF16)
    ones = jnp.ones((16, C), F32).astype(BF16)
    bsum[0] = (nt(ones, hi) + nt(ones, mid) + nt(ones, lo))[0:8]
    b1 = [copy(bsum.at[0], b1r.at[2 * a + b], B1 + 2 * a + b, peer(dx=a, ec=b)) for a, b in near]
    begin(b1)
    pass_slab(2)
    end(w2)
    part = wpart[...]
    for a, b in far:
        part = part + w2r[2 * a + b]
    wtot[wslice(wid(0, 0)), :] = part
    w3 = [
        copy(
            wtot.at[wslice(wid(0, 0))], wtot.at[wslice(wid(0, 0))], W3 + 2 * a + b,
            peer(dx=a, ec=b),
        )
        for a, b in near
    ]
    begin(w3)

    def dpair_row(j, _):
        dbj = dball[j]
        wq = wbt[pl.ds(pl.multiple_of(h * DH, DH), DH), :].astype(BF16)
        g = nn(wq, dbj.astype(BF16))
        first = jnp.sum(dbj * wbar, axis=0, keepdims=True)
        second = jnp.sum(dbj * braw[j], axis=0, keepdims=True) * (1.0 / C)
        dpair[j] = (rp[pl.ds(j, 1), :] * (g - first - yq[j] * second)).astype(BF16)
        return 0

    end(r5)
    for d in (1, 2, 3):
        dball[:, d, :] = r4[d].astype(F32)
    dball[:, 4:16, :] = jnp.zeros((OWN, 12, N), F32)
    lax.fori_loop(0, 8, dpair_row, 0, unroll=4)
    out_low = pltpu.make_async_copy(dpair.at[0:8], o_dpair.at[0:8], load.at[4])
    out_low.start()
    end(b1)
    part = bsum[0]
    for a, b in near:
        part = part + b1r[2 * a + b]
    bsum[1] = part
    b2 = [copy(bsum.at[1], b2r.at[2 * a + b], B2 + 2 * a + b, peer(dy=a, ez=b)) for a, b in far]
    begin(b2)
    pass_slab(3)
    lax.fori_loop(8, OWN, dpair_row, 0, unroll=4)
    out_high = pltpu.make_async_copy(dpair.at[8:16], o_dpair.at[8:16], load.at[5])
    out_high.start()
    end(w3)
    o_dw[...] = wtot[0:C, :]
    o_dwout[...] = wtot[C : C + DH, :]
    slab_out = [pltpu.make_async_copy(dsl.at[i], o_dslab.at[i], load.at[i]) for i in range(ROWS)]
    for i in range(ROWS):
        end_slab(i)
        slab_out[i].start()
    end(b2)
    part = bsum[1]
    for a, b in far:
        part = part + b2r[2 * a + b]
    o_dwb[...] = part[0:1, :]
    for cp in slab_out + [out_low, out_high]:
        cp.wait()


def scratch():
    v = pltpu.VMEM
    return [
        v((ROWS, N, C), BF16),
        v((OWN, N, C), BF16),
        v((ROWS, N, C), BF16),
        v((C, C), BF16),
        v((C, 16), F32),
        v((16, C), BF16),
        v((4, 2, 4, 2, OWN, N), BF16),
        v((4, 2, 4, 2, OWN, N), F32),
        v((OWN, C, N), BF16),
        v((OWN, OWN, N), F32),
        v((OWN, DH, N), F32),
        v((OWN, N), F32),
        v((OWN, N), F32),
        v((ROWS, C, N), F32),
        v((8, N), F32),
        v((ROWS, C, N), BF16),
        v((ROWS, 8, 64, 128), BF16),
        v((ROWS, 4, 2, 128, C), BF16),
        v((ROWS, C, 2 * N), BF16),
        v((ROWS, 4, 2, 128, C), F32),
        v((ROWS, 64, N), F32),
        v((ROWS, DH, N), F32),
        v((ROWS, DH, N), F32),
        v((2, 4, 4, OWN, N), BF16),
        v((2, 4, 4, OWN, N), BF16),
        v((2, 4, 4, OWN, N), BF16),
        v((2, 4, 4, OWN, HALF), BF16),
        v((2, 4, 4, OWN, HALF), BF16),
        v((2, 2, 4, OWN, HALF), BF16),
        v((2, 4, OWN, HALF), BF16),
        v((2, 4, OWN, HALF), BF16),
        v((2, OWN, N), BF16),
        v((4, OWN, N), BF16),
        v((OWN, OWN, N), F32),
        v((ROWS, 2, C, HALF), BF16),
        v((ROWS, 2, C, HALF), BF16),
        v((ROWS, C, HALF), BF16),
        v((ROWS, C, HALF), BF16),
        v((ROWS, 2, HALF, C), BF16),
        v((OWN, DH, N), BF16),
        v((192, C), F32),
        v((8, 24, C), F32),
        v((24, C), F32),
        v((8, 24, C), F32),
        v((192, C), F32),
        v((C, C), F32),
        v((2, 8, C), F32),
        v((8, 8, C), F32),
        v((8, 8, C), F32),
        pltpu.SemaphoreType.DMA((SEMS.count,)),
        pltpu.SemaphoreType.DMA((SEMS.count,)),
        pltpu.SemaphoreType.DMA((6,)),
    ]


def hand_on(*refs):
    outs, held, sem = refs[5:10], refs[10:15], refs[15]
    first, second = [], []
    for k in range(5):
        pieces = 4 if k < 2 else 1
        for q in range(pieces):
            size = held[k].shape[0] // pieces
            part = pl.ds(q * size, size)
            one = sem.at[0, 4 * k + q]
            two = sem.at[1, 4 * k + q]
            first.append(pltpu.make_async_copy(refs[k].at[part], held[k].at[part], one))
            second.append(pltpu.make_async_copy(held[k].at[part], outs[k].at[part], two))
    for cp in first:
        cp.start()
    for cp, then in zip(first, second):
        cp.wait()
        then.start()
    for cp in second:
        cp.wait()


def shards(slab, pair, pair_mask, w_qkvg, w_out, w_bias, d_out):
    wt = jnp.transpose(w_qkvg, (1, 2, 0)).reshape(C, C)
    vm = pl.BlockSpec(memory_space=pltpu.VMEM)
    anywhere = pl.BlockSpec(memory_space=pl.ANY)
    shapes = (
        jax.ShapeDtypeStruct((ROWS, 2, HALF, C), BF16),
        jax.ShapeDtypeStruct((OWN, DH, N), BF16),
        jax.ShapeDtypeStruct((C, C), F32),
        jax.ShapeDtypeStruct((DH, C), F32),
        jax.ShapeDtypeStruct((1, C), F32),
    )
    outs = pl.pallas_call(
        kernel,
        out_shape=shapes,
        in_specs=[anywhere, anywhere, vm, vm, vm, vm, anywhere],
        out_specs=(anywhere, anywhere, vm, vm, vm),
        scratch_shapes=scratch(),
        compiler_params=pltpu.CompilerParams(
            collective_id=0, has_side_effects=True, vmem_limit_bytes=60 * 1024 * 1024
        ),
    )(slab, pair, pair_mask, wt, w_out, w_bias.T, d_out)
    in_hbm = pl.BlockSpec(memory_space=pltpu.HBM)
    d_slab, d_pair, dw, dwout, dwb = pl.pallas_call(
        hand_on,
        out_shape=shapes,
        in_specs=[in_hbm] * 5,
        out_specs=(in_hbm,) * 5,
        scratch_shapes=[pltpu.VMEM(one.shape, one.dtype) for one in shapes]
        + [pltpu.SemaphoreType.DMA((2, 20))],
    )(*outs)
    return (
        d_slab.reshape(ROWS, N, C),
        jnp.swapaxes(d_pair, 1, 2),
        jnp.transpose(dw.reshape(4, DH, C), (2, 0, 1)),
        dwout,
        dwb.T,
    )


def solution(mesh):
    placed = (
        P("rows", None, None),
        P("rows", None, None),
        P("rows", None),
        P(None, None, "heads"),
        P("heads", None),
        P(),
        P("rows", None, None),
    )
    return jax.shard_map(
        shards,
        mesh=mesh,
        in_specs=placed,
        out_specs=(
            P("rows", None, None),
            P("rows", None, "heads"),
            P(None, None, "heads"),
            P("heads", None),
            P(None, "heads"),
        ),
        check_vma=False,
    )
```

```python
import jax
import jax.numpy as jnp
from jax import lax
from jax.experimental import pallas as pl
from jax.experimental.pallas import tpu as pltpu
from jax.sharding import PartitionSpec as P

MESH = pl.DeviceIdType.MESH
F32 = jnp.float32
BF16 = jnp.bfloat16
N = 1024
C = 128
DH = 32
ROWS = 4
OWN = 16
BLK = 256
HALF = 512
EPS = 1e-05
SCALE = 1.0 / DH**0.5


def nn(a, b):
    return lax.dot_general(a, b, (((1,), (0,)), ((), ())), preferred_element_type=F32)


def nt(a, b):
    return lax.dot_general(a, b, (((1,), (1,)), ((), ())), preferred_element_type=F32)


def norm_cols(t):
    cen = t - jnp.mean(t, axis=0, keepdims=True)
    r = lax.rsqrt(jnp.mean(cen * cen, axis=0, keepdims=True) + EPS)
    return cen * r, r


class Sems:
    def __init__(self):
        self.count = 0

    def take(self, n):
        first = self.count
        self.count += n
        return first


SEMS = Sems()
G1 = SEMS.take(1)
GP = SEMS.take(32)
GC = SEMS.take(2)
R1 = SEMS.take(2)
R2 = SEMS.take(16)
R3 = SEMS.take(16)
R4 = SEMS.take(4)
S1 = SEMS.take(8)
S2 = SEMS.take(4)
T1 = SEMS.take(8)
T2 = SEMS.take(4)
W1 = SEMS.take(8)
W2 = SEMS.take(8)
W3 = SEMS.take(8)
B1 = SEMS.take(8)
B2 = SEMS.take(8)
LOW = slice(0, HALF)
HIGH = slice(HALF, N)


def kernel(
    slab_h, pair_h, mask, wt, wout, wbias, dout_h,
    o_dslab, o_dpair, o_dw, o_dwout, o_dwb,
    slab, pair, dout, wn, wbt, wb,
    plane, dbias, xpt, braw, yq, rp, own_bias, ys, rs, xst, zq, z, rhs, natt,
    dkv, gate_s, do_s, s1, r1, s2, r2a, r2b, s3, r3a, r3b, s4, r4, dball,
    dxs, e1, dxc, e2, dsl, dpair, wacc, w1r, wpart, w2r, wtot, fold, bsum, b1r, b2r,
    send, recv, load,
):
    r = lax.axis_index("rows")
    h = lax.axis_index("heads")
    c = lax.rem(r, 2)
    x = lax.rem(r // 2, 4)
    zh = lax.rem(r // 8, 2)
    y = r // 16
    oz = 1 - zh
    inner = (h == 1) | (h == 2)
    at_end = jnp.logical_not(inner)
    side = h // 2
    mine = jnp.where(inner, h - 1, 0)
    to_inner = (r, jnp.where(inner, 3 - h, 1 + side))
    to_end = (r, jnp.where(h == 1, 0, 3))
    to_other = (r, 3 - h)

    def off(a, d):
        return lax.rem(a + d, 4)

    def flip(a, e):
        return 1 - a if e else a

    def peer(dy=0, ez=0, dx=0, ec=0, dh=0):
        row = ((off(y, dy) * 2 + flip(zh, ez)) * 4 + off(x, dx)) * 2 + flip(c, ec)
        return (row, off(h, dh))

    def copy(src, dst, sem, to):
        return pltpu.make_async_remote_copy(
            src_ref=src, dst_ref=dst, send_sem=send.at[sem], recv_sem=recv.at[sem],
            device_id=to, device_id_type=MESH,
        )

    loads = [pltpu.make_async_copy(pair_h.at[4 * k : 4 * k + 4], pair.at[4 * k : 4 * k + 4], load.at[k]) for k in range(4)]
    loads.append(pltpu.make_async_copy(slab_h, slab, load.at[4]))
    loads.append(pltpu.make_async_copy(dout_h, dout, load.at[5]))
    for cp in loads:
        cp.start()

    near = [(dx, ec) for dx in range(4) for ec in range(2) if dx or ec]
    far = [(dy, ez) for dy in range(4) for ez in range(2) if dy or ez]
    peers = [peer(dx=a, ec=b) for a, b in near] + [peer(dy=a, ez=b) for a, b in far]
    for d in (1, 2, 3):
        peers.append(peer(dh=d))
    barrier = pltpu.get_barrier_semaphore()
    for to in peers:
        pl.semaphore_signal(barrier, inc=1, device_id=to, device_id_type=MESH)

    eye = (
        lax.broadcasted_iota(jnp.int32, (C, C), 0) == lax.broadcasted_iota(jnp.int32, (C, C), 1)
    ).astype(F32).astype(BF16)

    wn[...] = nt(eye, wt[...]).astype(BF16)
    row16 = lax.broadcasted_iota(jnp.int32, (16, C), 0)
    heads = wbias[...].astype(F32)
    wrel = jnp.zeros((16, C), F32)
    for k in range(4):
        wrel = wrel + jnp.where(row16 == off(h + 4, -k), heads[k : k + 1, :], 0.0)
    wb[...] = wrel.astype(BF16)
    wbt[...] = nt(eye, wrel.astype(BF16))
    wbar = jnp.mean(wrel, axis=1, keepdims=True)

    def pair_row(j, _):
        yt, rj = norm_cols(nt(eye, pair[j]))
        xb = yt.astype(BF16)
        xpt[j] = xb
        rp[pl.ds(j, 1), :] = rj
        ys[lax.rem(j, 2)] = yt
        yq[j] = ys[lax.rem(j, 2), pl.ds(pl.multiple_of(h * DH, DH), DH), :]
        raw = nn(wb[...], xb)
        braw[j] = raw
        own_bias[pl.ds(j, 1), :] = raw[0:1, :]
        return 0

    for k in range(4):
        loads[k].wait()
        lax.fori_loop(4 * k, 4 * k + 4, pair_row, 0, unroll=True)
    plane[y, zh, x, c] = own_bias[...].astype(BF16)
    pl.semaphore_wait(barrier, len(peers))

    def gather_first(s):
        zs = flip(zh, s)
        out = []
        for d in (1, 2, 3):
            low = plane.at[y, zs, x, c, :, LOW]
            high = plane.at[y, zs, x, c, :, HIGH]
            out.append(copy(low, low, GP + 16 * s + d, peer(dx=d)))
            out.append(copy(high, high, GP + 16 * s + 4 + d, peer(dy=d)))
        return out

    def gather_second(s):
        zs = flip(zh, s)
        out = []
        for d in (1, 2, 3):
            low = plane.at[y, zs, :, c, :, LOW]
            high = plane.at[:, zs, x, c, :, HIGH]
            out.append(copy(low, low, GP + 16 * s + 8 + d, peer(dy=d)))
            out.append(copy(high, high, GP + 16 * s + 12 + d, peer(dx=d)))
        return out

    def gather_core(s):
        zs = flip(zh, s)
        return copy(plane.at[:, zs, :, c], plane.at[:, zs, :, c], GC + s, peer(ec=1))

    def begin(copies):
        for cp in copies:
            cp.start()

    def end(copies):
        for cp in copies:
            cp.wait()

    g1 = copy(plane.at[y, zh, x, c], plane.at[y, zh, x, c], G1, peer(ez=1))
    g1.start()
    ga1 = gather_first(0)
    begin(ga1)

    def slab_row(i, _):
        yt, ri = norm_cols(nt(eye, slab[i]))
        ys[i] = yt
        rs[pl.ds(i, 1), :] = ri
        xb = yt.astype(BF16)
        xst[i] = xb
        proj = nn(wt[...], xb)
        gate = 1.0 / (1.0 + jnp.exp(-proj[96:128]))
        do = nt(wout[...], dout[i])
        gate_s[i] = gate
        do_s[i] = do
        datt = do * gate
        stack = jnp.concatenate([proj[0:96], datt], axis=0)
        z[i] = stack.T.astype(BF16).reshape(4, 2, 128, C)
        both = jnp.concatenate([proj[0:DH], datt], axis=0).astype(BF16)
        for k in range(8):
            zq[i, k] = both[:, k * 128 : (k + 1) * 128]
        rhs[i, 0:DH, 0:N] = proj[32:64].astype(BF16)
        rhs[i, 96:128, N : 2 * N] = proj[64:96].astype(BF16)
        return 0

    rhs[...] = jnp.zeros(rhs.shape, BF16)
    loads[4].wait()
    loads[5].wait()
    lax.fori_loop(0, 2, slab_row, 0)
    end(ga1)
    ga2 = gather_second(0)
    begin(ga2)
    g1.wait()
    gb1 = gather_first(1)
    begin(gb1)
    lax.fori_loop(2, ROWS, slab_row, 0)
    wacc[...] = jnp.zeros(wacc.shape, F32)
    dkv[...] = jnp.zeros(dkv.shape, F32)
    dbias[...] = jnp.zeros(dbias.shape, F32)
    end(gb1)
    gb2 = gather_second(1)
    begin(gb2)
    end(ga2)
    gac = gather_core(0)
    gac.start()
    gac.wait()

    def block(i, zs):
        keep = mask[pl.ds(i, 1), :] == 1
        zj = z[i, :, zs].reshape(HALF, C)
        bias = plane[:, zs].reshape(HALF, N).astype(F32)
        logits = nn(zj[:, 0:DH], rhs[i, 0:DH, 0:N]) * SCALE + bias
        logits = jnp.where(keep, logits, -1e9)
        expo = jnp.exp(logits - jnp.max(logits, axis=1, keepdims=True))
        probs = expo * (1.0 / jnp.sum(expo, axis=1, keepdims=True))
        pb = probs.astype(BF16)
        dp = nn(zj[:, 96:128], rhs[i, 96:128, N : 2 * N])
        dl = probs * (dp - jnp.sum(probs * dp, axis=1, keepdims=True))
        dl = jnp.where(keep, dl, 0.0)
        dlb = dl.astype(BF16)
        dbias[:, zs] += dl.reshape(4, 4, 2, OWN, N)
        zall = z[i].reshape(N, C)
        lane = lax.broadcasted_iota(jnp.int32, (HALF, C), 1)
        nat = jnp.where(lane < 64, nn(dlb, zall), nn(pb, zall))
        natt[i, :, zs] = nat.reshape(4, 128, C)
        left = jnp.concatenate([zq[i, 2 * k + zs] for k in range(4)], axis=1)
        dkv[i, 0:DH, :] += nn(left[0:DH], dlb)
        dkv[i, DH:64, :] += nn(left[DH:64], pb)

    def up_copies(i):
        far_half = 1 - side
        return [
            copy(dxs.at[i, far_half], e1.at[i, far_half], S1 + 2 * i, to_inner),
            copy(dxs.at[i, side], e1.at[i, side], S1 + 2 * i + 1, to_inner),
        ]

    def cross_copy(i):
        return copy(dxc.at[i], e2.at[i], S2 + i, to_other)

    def done_copies(i):
        return [
            copy(dsl.at[i, mine], dsl.at[i, mine], T1 + 2 * i, to_other),
            copy(dsl.at[i, mine], dsl.at[i, mine], T1 + 2 * i + 1, to_end),
        ]

    def pass_copy(i):
        return copy(dsl.at[i, 1 - mine], dsl.at[i, 1 - mine], T2 + i, to_end)

    def send_row(i):
        @pl.when(at_end)
        def _():
            begin(up_copies(i))

    def middle_slab(i):
        @pl.when(inner)
        def _():
            up_copies(i)[0].wait_recv()
            g = dxs[i, 1 - mine].astype(F32) + e1[i, 1 - mine].astype(F32)
            dxc[i] = g.astype(BF16)
            cross_copy(i).start()

    def finish_slab(i):
        @pl.when(inner)
        def _():
            up_copies(i)[1].wait_recv()
            cross_copy(i).wait()
            g = dxs[i, mine].astype(F32) + e1[i, mine].astype(F32) + e2[i].astype(F32)
            cols = pl.ds(pl.multiple_of(mine * HALF, HALF), HALF)
            yt = ys[i, :, cols]
            ri = rs[pl.ds(i, 1), cols]
            first = jnp.mean(g, axis=0, keepdims=True)
            out = ri * (g - first - yt * jnp.mean(g * yt, axis=0, keepdims=True))
            dsl[i, mine] = out.T.astype(BF16)
            begin(done_copies(i))

    def pass_slab(i):
        @pl.when(inner)
        def _():
            done_copies(i)[0].wait_recv()
            pass_copy(i).start()

    def end_slab(i):
        @pl.when(inner)
        def _():
            for cp in done_copies(i) + [pass_copy(i)]:
                cp.wait_send()

        @pl.when(at_end)
        def _():
            for cp in up_copies(i):
                cp.wait_send()
            done_copies(i)[1].wait_recv()
            pass_copy(i).wait_recv()

    def finish_row(i):
        nat = natt[i].reshape(N, C).T
        gate = gate_s[i]
        do = do_s[i]
        att = nat[64:96]
        gated = (gate * att).astype(BF16)
        dgate = do * att * gate * (1.0 - gate)
        grads = jnp.concatenate(
            [nat[32:64] * SCALE, dkv[i, 0:DH, :] * SCALE, dkv[i, DH:64, :], dgate], axis=0
        ).astype(BF16)
        dx = nn(wn[...], grads).astype(BF16)
        dxs[i, 0] = dx[:, LOW]
        dxs[i, 1] = dx[:, HIGH]
        send_row(i)
        wacc[0:C, :] += nt(grads, xst[i])
        wacc[C : C + DH, :] += nn(gated, dout[i])

    def sum_core(s):
        zs = flip(zh, s)
        s1[s] = dbias[:, zs, :, 1 - c].astype(BF16)
        return copy(s1.at[s], r1.at[s], R1 + s, peer(ec=1))

    def sum_first(s):
        zs = flip(zh, s)
        for yy in range(4):
            total = dbias[yy, zs, :, c] + r1[s, yy].astype(F32)
            dbias[yy, zs, :, c] = total
            s2[s, yy] = total.astype(BF16)
        out = []
        for d in (1, 2, 3):
            low = s2.at[s, off(y, d), :, :, LOW]
            high = s2.at[s, :, off(x, d), :, HIGH]
            out.append(copy(low, r2a.at[s, d], R2 + 8 * s + d, peer(dy=d)))
            out.append(copy(high, r2b.at[s, d], R2 + 8 * s + 4 + d, peer(dx=d)))
        return out

    def sum_second(s):
        zs = flip(zh, s)
        low = dbias[y, zs, :, c, :, LOW]
        high = dbias[:, zs, x, c, :, HIGH]
        for d in (1, 2, 3):
            low = low + r2a[s, d].astype(F32)
            high = high + r2b[s, d].astype(F32)
        s3[s, 0] = low.astype(BF16)
        s3[s, 1] = high.astype(BF16)
        dbias[y, zs, :, c, :, LOW] = low
        dbias[:, zs, x, c, :, HIGH] = high
        out = []
        for d in (1, 2, 3):
            out.append(copy(s3.at[s, 0, off(x, d)], r3a.at[s, d], R3 + 8 * s + d, peer(dx=d)))
            out.append(copy(s3.at[s, 1, off(y, d)], r3b.at[s, d], R3 + 8 * s + 4 + d, peer(dy=d)))
        return out

    def sum_last(s):
        zs = flip(zh, s)
        low = dbias[y, zs, x, c, :, LOW]
        high = dbias[y, zs, x, c, :, HIGH]
        for d in (1, 2, 3):
            low = low + r3a[s, d].astype(F32)
            high = high + r3b[s, d].astype(F32)
        return jnp.concatenate([low, high], axis=1)

    def own_row(i):
        block(i, zh)

    def other_row(i):
        block(i, oz)

    own_row(0)
    own_row(1)
    end(gb2)
    gbc = gather_core(1)
    gbc.start()
    own_row(2)
    gbc.wait()
    for i in range(3):
        other_row(i)
        finish_row(i)
    own_row(3)
    ra1 = sum_core(0)
    ra1.start()
    middle_slab(0)
    other_row(3)
    rb1 = sum_core(1)
    rb1.start()
    finish_row(3)
    chunk = 24

    def wslice(k):
        return pl.ds(pl.multiple_of(k * chunk, 8), chunk)

    def wid(dx, ec):
        return off(x, dx) * 2 + flip(c, ec)

    w1 = [
        copy(wacc.at[wslice(wid(a, b))], w1r.at[2 * a + b], W1 + 2 * a + b, peer(dx=a, ec=b))
        for a, b in near
    ]
    rb1.wait()
    rb2 = sum_first(1)
    begin(rb2)
    begin(w1)
    middle_slab(1)
    finish_slab(0)
    ra1.wait()
    ra2 = sum_first(0)
    end(rb2)
    rb3 = sum_second(1)
    begin(rb3)
    begin(ra2)
    middle_slab(2)
    finish_slab(1)
    pass_slab(0)
    end(w1)
    part = wacc[wslice(wid(0, 0)), :]
    for a, b in near:
        part = part + w1r[2 * a + b]
    wpart[...] = part
    w2 = [copy(wpart, w2r.at[2 * a + b], W2 + 2 * a + b, peer(dy=a, ez=b)) for a, b in far]
    begin(w2)
    end(rb3)
    s4[1] = sum_last(1).astype(BF16)
    rb4 = copy(s4.at[1], r4.at[0], R4, peer(ez=1))
    rb4.start()
    middle_slab(3)
    finish_slab(2)
    pass_slab(1)
    end(ra2)
    ra3 = sum_second(0)
    begin(ra3)
    end(ra3)
    own = sum_last(0)
    rb4.wait()

    db = own + r4[0].astype(F32)
    s4[0] = db.astype(BF16)
    r5 = [copy(s4.at[0], r4.at[d], R4 + d, peer(dh=d)) for d in (1, 2, 3)]
    begin(r5)
    own_bias[...] = db
    dball[:, 0, :] = db

    def wb_part(k, _):
        sub = pl.ds(pl.multiple_of(k * 32, 32), 32)
        acc = xpt[0, sub, :].astype(F32) * own_bias[0:1, :]
        for j in range(1, OWN):
            acc = acc + xpt[j, sub, :].astype(F32) * own_bias[j : j + 1, :]
        total = acc[:, 0:128]
        for q in range(1, 8):
            total = total + acc[:, q * 128 : (q + 1) * 128]
        fold[sub, :] = total
        return 0

    lax.fori_loop(0, 4, wb_part, 0)
    total = fold[...]
    hi = total.astype(BF16)
    mid = (total - hi.astype(F32)).astype(BF16)
    lo = (total - hi.astype(F32) - mid.astype(F32)).astype(BF16)
    ones = jnp.ones((16, C), F32).astype(BF16)
    bsum[0] = (nt(ones, hi) + nt(ones, mid) + nt(ones, lo))[0:8]
    b1 = [copy(bsum.at[0], b1r.at[2 * a + b], B1 + 2 * a + b, peer(dx=a, ec=b)) for a, b in near]
    begin(b1)
    finish_slab(3)
    pass_slab(2)
    end(w2)
    part = wpart[...]
    for a, b in far:
        part = part + w2r[2 * a + b]
    wtot[wslice(wid(0, 0)), :] = part
    w3 = [
        copy(
            wtot.at[wslice(wid(0, 0))], wtot.at[wslice(wid(0, 0))], W3 + 2 * a + b,
            peer(dx=a, ec=b),
        )
        for a, b in near
    ]
    begin(w3)

    def dpair_row(j, _):
        dbj = dball[j]
        wq = wbt[pl.ds(pl.multiple_of(h * DH, DH), DH), :].astype(BF16)
        g = nn(wq, dbj.astype(BF16))
        first = jnp.sum(dbj * wbar, axis=0, keepdims=True)
        second = jnp.sum(dbj * braw[j], axis=0, keepdims=True) * (1.0 / C)
        dpair[j] = (rp[pl.ds(j, 1), :] * (g - first - yq[j] * second)).astype(BF16)
        return 0

    end(r5)
    for d in (1, 2, 3):
        dball[:, d, :] = r4[d].astype(F32)
    dball[:, 4:16, :] = jnp.zeros((OWN, 12, N), F32)
    lax.fori_loop(0, 8, dpair_row, 0, unroll=4)
    out_low = pltpu.make_async_copy(dpair.at[0:8], o_dpair.at[0:8], load.at[4])
    out_low.start()
    end(b1)
    part = bsum[0]
    for a, b in near:
        part = part + b1r[2 * a + b]
    bsum[1] = part
    b2 = [copy(bsum.at[1], b2r.at[2 * a + b], B2 + 2 * a + b, peer(dy=a, ez=b)) for a, b in far]
    begin(b2)
    pass_slab(3)
    lax.fori_loop(8, OWN, dpair_row, 0, unroll=4)
    out_high = pltpu.make_async_copy(dpair.at[8:16], o_dpair.at[8:16], load.at[5])
    out_high.start()
    end(w3)
    o_dw[...] = wtot[0:C, :]
    o_dwout[...] = wtot[C : C + DH, :]
    slab_out = [pltpu.make_async_copy(dsl.at[i], o_dslab.at[i], load.at[i]) for i in range(ROWS)]
    for i in range(ROWS):
        end_slab(i)
        slab_out[i].start()
    end(b2)
    part = bsum[1]
    for a, b in far:
        part = part + b2r[2 * a + b]
    o_dwb[...] = part[0:1, :]
    for cp in slab_out + [out_low, out_high]:
        cp.wait()


def scratch():
    v = pltpu.VMEM
    return [
        v((ROWS, N, C), BF16),
        v((OWN, N, C), BF16),
        v((ROWS, N, C), BF16),
        v((C, C), BF16),
        v((C, 16), F32),
        v((16, C), BF16),
        v((4, 2, 4, 2, OWN, N), BF16),
        v((4, 2, 4, 2, OWN, N), F32),
        v((OWN, C, N), BF16),
        v((OWN, OWN, N), F32),
        v((OWN, DH, N), F32),
        v((OWN, N), F32),
        v((OWN, N), F32),
        v((ROWS, C, N), F32),
        v((8, N), F32),
        v((ROWS, C, N), BF16),
        v((ROWS, 8, 64, 128), BF16),
        v((ROWS, 4, 2, 128, C), BF16),
        v((ROWS, C, 2 * N), BF16),
        v((ROWS, 4, 2, 128, C), F32),
        v((ROWS, 64, N), F32),
        v((ROWS, DH, N), F32),
        v((ROWS, DH, N), F32),
        v((2, 4, 4, OWN, N), BF16),
        v((2, 4, 4, OWN, N), BF16),
        v((2, 4, 4, OWN, N), BF16),
        v((2, 4, 4, OWN, HALF), BF16),
        v((2, 4, 4, OWN, HALF), BF16),
        v((2, 2, 4, OWN, HALF), BF16),
        v((2, 4, OWN, HALF), BF16),
        v((2, 4, OWN, HALF), BF16),
        v((2, OWN, N), BF16),
        v((4, OWN, N), BF16),
        v((OWN, OWN, N), F32),
        v((ROWS, 2, C, HALF), BF16),
        v((ROWS, 2, C, HALF), BF16),
        v((ROWS, C, HALF), BF16),
        v((ROWS, C, HALF), BF16),
        v((ROWS, 2, HALF, C), BF16),
        v((OWN, DH, N), BF16),
        v((192, C), F32),
        v((8, 24, C), F32),
        v((24, C), F32),
        v((8, 24, C), F32),
        v((192, C), F32),
        v((C, C), F32),
        v((2, 8, C), F32),
        v((8, 8, C), F32),
        v((8, 8, C), F32),
        pltpu.SemaphoreType.DMA((SEMS.count,)),
        pltpu.SemaphoreType.DMA((SEMS.count,)),
        pltpu.SemaphoreType.DMA((6,)),
    ]


def hand_on(*refs):
    outs, held, sem = refs[5:10], refs[10:15], refs[15]
    first, second = [], []
    for k in range(5):
        pieces = 4 if k < 2 else 1
        for q in range(pieces):
            size = held[k].shape[0] // pieces
            part = pl.ds(q * size, size)
            one = sem.at[0, 4 * k + q]
            two = sem.at[1, 4 * k + q]
            first.append(pltpu.make_async_copy(refs[k].at[part], held[k].at[part], one))
            second.append(pltpu.make_async_copy(held[k].at[part], outs[k].at[part], two))
    for cp in first:
        cp.start()
    for cp, then in zip(first, second):
        cp.wait()
        then.start()
    for cp in second:
        cp.wait()


def shards(slab, pair, pair_mask, w_qkvg, w_out, w_bias, d_out):
    wt = jnp.transpose(w_qkvg, (1, 2, 0)).reshape(C, C)
    vm = pl.BlockSpec(memory_space=pltpu.VMEM)
    anywhere = pl.BlockSpec(memory_space=pl.ANY)
    shapes = (
        jax.ShapeDtypeStruct((ROWS, 2, HALF, C), BF16),
        jax.ShapeDtypeStruct((OWN, DH, N), BF16),
        jax.ShapeDtypeStruct((C, C), F32),
        jax.ShapeDtypeStruct((DH, C), F32),
        jax.ShapeDtypeStruct((1, C), F32),
    )
    outs = pl.pallas_call(
        kernel,
        out_shape=shapes,
        in_specs=[anywhere, anywhere, vm, vm, vm, vm, anywhere],
        out_specs=(anywhere, anywhere, vm, vm, vm),
        scratch_shapes=scratch(),
        compiler_params=pltpu.CompilerParams(
            collective_id=0, has_side_effects=True, vmem_limit_bytes=60 * 1024 * 1024
        ),
    )(slab, pair, pair_mask, wt, w_out, w_bias.T, d_out)
    in_hbm = pl.BlockSpec(memory_space=pltpu.HBM)
    d_slab, d_pair, dw, dwout, dwb = pl.pallas_call(
        hand_on,
        out_shape=shapes,
        in_specs=[in_hbm] * 5,
        out_specs=(in_hbm,) * 5,
        scratch_shapes=[pltpu.VMEM(one.shape, one.dtype) for one in shapes]
        + [pltpu.SemaphoreType.DMA((2, 20))],
    )(*outs)
    return (
        d_slab.reshape(ROWS, N, C),
        jnp.swapaxes(d_pair, 1, 2),
        jnp.transpose(dw.reshape(4, DH, C), (2, 0, 1)),
        dwout,
        dwb.T,
    )


def solution(mesh):
    placed = (
        P("rows", None, None),
        P("rows", None, None),
        P("rows", None),
        P(None, None, "heads"),
        P("heads", None),
        P(),
        P("rows", None, None),
    )
    return jax.shard_map(
        shards,
        mesh=mesh,
        in_specs=placed,
        out_specs=(
            P("rows", None, None),
            P("rows", None, "heads"),
            P(None, None, "heads"),
            P("heads", None),
            P(None, "heads"),
        ),
        check_vma=False,
    )
```
